256 devices in a mesh: prow: 8 (over x_lo, y), pcol: 32 (over z, x_hi, core).
Axes of the slice: x: 4 (x_hi: 2, x_lo: 2; x = x_hi * 2 + x_lo), y: 4, z: 8, core: 2. Of those that a mesh axis runs over, the one named last changes fastest.
Arguments:
- panels: bfloat16 [16384, 256], P(('prow', 'pcol')), may hold values from -2 to 42, as said below
- pivots: int32 [2, 128], replicated, may hold values from 0 to 16383, as said below
- trailing: bfloat16 [16384, 32768], P('prow', 'pcol'), may hold values from -6 to 6
Outputs:
- updated: bfloat16 [16384, 32768], P('prow', 'pcol')
- upper_rows: bfloat16 [256, 32768], P(None, 'pcol')
The draws below stay inside these ranges and needn't reach their ends.
Inputs may be any that keep to these rules, and one draw needn't show every extreme that they name: `pivots`: the 256 pivot rows are distinct; every aligned block of 64 rows holds the same number of them. `panels`: the entry of row pivots[p, i] in column p * 128 + i is 38 or more; every other entry lies within 2 of zero.
All inputs are finite; a program needn't handle non-finite values.
Results may differ from the reference program's by a relative error of at most 0.039.
Values may be sent and summed in bfloat16 or wider, within the bound.
A program may use at most 64 MiB of HBM per device.

```python
import jax
import jax.numpy as jnp
from jax import lax

NB = 128
ROWS_DEV = 64
ROWS = 16384
COLUMNS = 32768
N_PROW = 8
N_PCOL = 32


def pivot_table(key):
    key = jax.random.fold_in(key, 11)
    key_offsets, key_target, key_slots = jax.random.split(key, 3)
    devices = N_PROW * N_PCOL
    per_device = 2 * NB // devices

    def row_offsets(sub_key):
        return jax.random.permutation(sub_key, ROWS_DEV)[:per_device]
    offsets = jax.vmap(row_offsets)(jax.random.split(key_offsets, devices))
    target = jax.random.randint(key_target, (devices,), 0, ROWS_DEV)
    target = target.at[0].set(0).at[devices - 1].set(ROWS_DEV - 1)
    offsets = (offsets - offsets[:, :1] + target[:, None]) % ROWS_DEV
    rows_all = jnp.arange(devices, dtype=jnp.int32)[:, None] * ROWS_DEV + offsets
    slot_order = jax.random.permutation(key_slots, 2 * NB)
    return rows_all.reshape(-1)[slot_order].reshape(2, NB).astype(jnp.int32)


def draw_pivots(key, part):
    return pivot_table(key)


def draw_panels(key, part):
    table = pivot_table(key)
    key = jax.random.fold_in(key, 5)
    values = jax.random.uniform(key, (ROWS, 2 * NB), jnp.float32, -2.0, 2.0)
    values = values.at[table.reshape(-1), jnp.arange(2 * NB)].add(40.0)
    return values.astype(jnp.bfloat16)


def block_scale(stream_key, shape, pieces, least, largest):
    def one(axis_at, parts):
        steps = jax.random.uniform(jax.random.fold_in(jax.random.fold_in(stream_key, 6), axis_at), (parts,), jnp.float32, least / len(pieces), largest / len(pieces))
        return jnp.repeat(jnp.exp(steps), shape[axis_at] // parts).reshape((-1,) + (1,) * (len(shape) - axis_at - 1))

    gain = one(*pieces[0])
    for cut in pieces[1:]:
        gain = gain * one(*cut)
    return gain


def noise(key, shape, scale, limit, shards=(), held_as=jnp.bfloat16):
    drawn = scale * jax.random.normal(key, shape, jnp.float32)
    if shards:
        drawn = drawn * block_scale(key, shape, shards, -0.22, 0.18)
    return jnp.clip(drawn, -limit, limit).astype(held_as)


def setup_inputs(seed: int = 0) -> dict:
    streams_of = jax.random.split(jax.random.key(seed), 4)
    panels = draw_panels(jax.random.fold_in(streams_of[3], 71), 0)
    pivots = draw_pivots(jax.random.fold_in(streams_of[3], 71), 0)
    trailing = noise(streams_of[2], (ROWS, COLUMNS), 1.0, 6.0, ((0, 8), (1, 32)))
    return dict(panels=panels, pivots=pivots, trailing=trailing)


def exact_dot(left, right):
    return jnp.dot(left, right, precision=lax.Precision.HIGHEST)


def factor_packed(matrix):
    extent = matrix.shape[0]
    index_all = jnp.arange(extent, dtype=jnp.int32)

    def elimination(pivot_step, current):
        step_now = jnp.asarray(pivot_step).astype(jnp.int32)
        column = lax.dynamic_slice_in_dim(current, step_now, 1, 1)[:, 0]
        pivot_row = lax.dynamic_slice_in_dim(current, step_now, 1, 0)[0]
        pivot_value = lax.dynamic_slice_in_dim(column, step_now, 1, 0)[0]
        below = index_all > step_now
        factor = jnp.where(below, column / pivot_value, jnp.zeros_like(column))
        right_part = jnp.where(below, pivot_row, jnp.zeros_like(pivot_row))
        current = current - factor[:, None] * right_part[None, :]
        place = below[:, None] & (index_all[None, :] == step_now)
        return jnp.where(place, factor[:, None], current)

    return lax.fori_loop(0, extent - 1, elimination, matrix)


def nilpotent_inverse(strict):
    extent = strict.shape[0]
    identity = jnp.eye(extent, dtype=jnp.float32)
    powered = strict
    result = identity - strict
    for _ in range((extent - 1).bit_length() - 1):
        powered = exact_dot(powered, powered)
        result = exact_dot(result, identity + powered)
    return result


def triangular_inverses(packed):
    diagonal = jnp.diagonal(packed)
    inv_lower = nilpotent_inverse(jnp.tril(packed, -1))
    inv_upper = nilpotent_inverse(jnp.triu(packed, 1) / diagonal[:, None]) / diagonal[None, :]
    return inv_lower, inv_upper


def pivot_factors(picked):
    panel_width = picked.shape[0] // 2
    inv_lower_one, inv_upper_one = triangular_inverses(factor_packed(picked[:panel_width, :panel_width]))
    cross_upper = exact_dot(inv_lower_one, picked[:panel_width, panel_width:]).astype(jnp.bfloat16)
    left_pivots = exact_dot(picked[panel_width:, :panel_width], inv_upper_one).astype(jnp.bfloat16)
    second_block = picked[panel_width:, panel_width:] - jnp.dot(left_pivots, cross_upper, preferred_element_type=jnp.float32)
    inv_lower_two, inv_upper_two = triangular_inverses(factor_packed(second_block))
    return inv_lower_one, inv_upper_one, cross_upper, left_pivots, inv_lower_two, inv_upper_two


def panel_rows(raw_rows, inv_upper_one, cross_upper, inv_upper_two):
    panel_width = cross_upper.shape[0]
    lower_one = exact_dot(raw_rows[:, :panel_width].astype(jnp.float32), inv_upper_one).astype(jnp.bfloat16)
    second_cols = raw_rows[:, panel_width:].astype(jnp.float32) - jnp.dot(lower_one, cross_upper, preferred_element_type=jnp.float32)
    lower_two = exact_dot(second_cols, inv_upper_two).astype(jnp.bfloat16)
    return jnp.concatenate([lower_one, lower_two], axis=1)


def upper_solve(chosen, inv_lower_one, left_pivots, inv_lower_two):
    panel_width = left_pivots.shape[0]
    upper_one = exact_dot(inv_lower_one, chosen[:panel_width]).astype(jnp.bfloat16)
    inner = chosen[panel_width:] - jnp.dot(left_pivots, upper_one, preferred_element_type=jnp.float32)
    upper_two = exact_dot(inv_lower_two, inner).astype(jnp.bfloat16)
    return jnp.concatenate([upper_one, upper_two], axis=0)


def reference(panels, pivots, trailing):
    flat_piv = pivots.reshape(-1).astype(jnp.int32)
    picked = jnp.take(panels, flat_piv, axis=0).astype(jnp.float32)
    inv_lower_one, inv_upper_one, cross_upper, left_pivots, inv_lower_two, inv_upper_two = pivot_factors(picked)
    factors = panel_rows(panels, inv_upper_one, cross_upper, inv_upper_two)
    chosen = jnp.take(trailing, flat_piv, axis=0).astype(jnp.float32)
    upper_rows = upper_solve(chosen, inv_lower_one, left_pivots, inv_lower_two)
    block_count = trailing.shape[0] // ROWS_DEV
    slab_blocks = trailing.reshape(block_count, ROWS_DEV, trailing.shape[1])
    factor_blocks = factors.reshape(block_count, ROWS_DEV, factors.shape[1])

    def update_block(pair_rows):
        slab_rows, factor_rows = pair_rows
        return (slab_rows.astype(jnp.float32) - jnp.dot(factor_rows, upper_rows, preferred_element_type=jnp.float32)).astype(jnp.bfloat16)

    updated = lax.map(update_block, (slab_blocks, factor_blocks)).reshape(trailing.shape)
    return updated, upper_rows
```

```python
import functools

import jax
import jax.numpy as jnp
from jax import lax
from jax.experimental import pallas as pl
from jax.experimental.pallas import tpu as pltpu
from jax.sharding import PartitionSpec as P

f32, bf16, i32 = jnp.float32, jnp.bfloat16, jnp.int32
MESH = pl.DeviceIdType.MESH
T_PARTS = 4
OUT_PARTS = 8


def split(x):
    high = x.astype(bf16)
    return high, (x - high.astype(f32)).astype(bf16)


def gather_kernel(
    n_prow, n_pcol, pivots, panels, trailing, g_out, c_out, p_out, t_buf, rows_buf,
    t_sem, s1_send, s1_recv, z_send, z_recv, x_send, x_recv, sib_send, sib_recv,
    g_send, g_recv, c_send, c_recv,
):
    n_z = n_pcol // 4
    prow, pcol = lax.axis_index("prow"), lax.axis_index("pcol")
    z, place = pcol // 4, lax.rem(pcol, 4)
    x_hi, core = place // 2, lax.rem(place, 2)
    rows_dev = panels.shape[0]
    part_rows = trailing.shape[0] // T_PARTS

    def t_copy(q):
        at = pl.ds(q * part_rows, part_rows)
        return pltpu.make_async_copy(trailing.at[at], t_buf.at[at], t_sem.at[q])

    for q in range(T_PARTS):
        t_copy(q).start()

    barrier = pltpu.get_barrier_semaphore()

    @pl.loop(1, n_pcol)
    def _(step):
        pl.semaphore_signal(
            barrier, inc=1, device_id={"pcol": lax.rem(pcol + step, n_pcol)}, device_id_type=MESH
        )

    @pl.loop(1, n_prow)
    def _(step):
        pl.semaphore_signal(
            barrier, inc=1, device_id={"prow": lax.rem(prow + step, n_prow)}, device_id_type=MESH
        )

    block = pivots[...] // rows_dev
    offset = pivots[...] - block * rows_dev
    offset_f = offset.astype(f32)
    own = jnp.where(block == prow * n_pcol + pcol, offset_f, 0.0)
    own_offset = jnp.sum(jnp.sum(own, axis=0, keepdims=True), axis=1, keepdims=True)
    lane = lax.broadcasted_iota(i32, (16, rows_dev), 1).astype(f32)
    pick = jnp.where(lane == own_offset, 1.0, 0.0).astype(bf16)
    own_row = jnp.dot(pick, panels[...], preferred_element_type=f32)
    rows_buf[pcol] = own_row[0:1, :]
    p_out[z, place] = panels[...]
    sub = lax.broadcasted_iota(i32, (n_pcol, pivots.shape[1]), 0) + prow * n_pcol
    found = jnp.where(block[0:1, :] == sub, offset_f[0:1, :], 0.0) + jnp.where(
        block[1:2, :] == sub, offset_f[1:2, :], 0.0
    )
    row_at = jnp.sum(found, axis=1, keepdims=True) + (
        lax.broadcasted_iota(i32, (n_pcol, 1), 0) * rows_dev
    ).astype(f32)

    pl.semaphore_wait(barrier, n_pcol - 1 + n_prow - 1)

    def s1_copy(source, target):
        return pltpu.make_async_remote_copy(
            src_ref=rows_buf.at[source], dst_ref=rows_buf.at[source],
            send_sem=s1_send.at[target], recv_sem=s1_recv.at[source],
            device_id={"pcol": target}, device_id_type=MESH,
        )

    @pl.loop(1, n_pcol)
    def _(step):
        s1_copy(pcol, lax.rem(pcol + step, n_pcol)).start()

    def z_copy(source, target):
        return pltpu.make_async_remote_copy(
            src_ref=p_out.at[source, place], dst_ref=p_out.at[source, place],
            send_sem=z_send.at[target], recv_sem=z_recv.at[source],
            device_id={"pcol": target * 4 + place}, device_id_type=MESH,
        )

    def x_copy(at_z, at_place):
        return pltpu.make_async_remote_copy(
            src_ref=p_out.at[at_z, at_place], dst_ref=p_out.at[at_z, at_place],
            send_sem=x_send.at[at_z], recv_sem=x_recv.at[at_z],
            device_id={"pcol": z * 4 + (1 - x_hi) * 2 + core}, device_id_type=MESH,
        )

    def sib_copy(slot, at_place):
        return pltpu.make_async_remote_copy(
            src_ref=p_out.at[:, at_place], dst_ref=p_out.at[:, at_place],
            send_sem=sib_send.at[slot], recv_sem=sib_recv.at[slot],
            device_id={"pcol": z * 4 + x_hi * 2 + (1 - core)}, device_id_type=MESH,
        )

    def z_at(step):
        half = (step + 1) // 2
        return lax.rem(z + n_z + jnp.where(lax.rem(step, 2) == 1, half, -half), n_z)

    @pl.loop(1, n_z)
    def _(step):
        z_copy(z, z_at(step)).start()

    x_copy(z, place).start()

    chosen = jnp.zeros((n_pcol, trailing.shape[1]), f32)
    for q in range(T_PARTS):
        t_copy(q).wait()
        lane = lax.broadcasted_iota(i32, (n_pcol, part_rows), 1).astype(f32) + q * part_rows
        pick = jnp.where(lane == row_at, 1.0, 0.0).astype(bf16)
        chosen = chosen + jnp.dot(
            pick, t_buf[q * part_rows:(q + 1) * part_rows, :], preferred_element_type=f32
        )
    own_rows = pl.ds(pl.multiple_of(prow * n_pcol, n_pcol), n_pcol)
    c_out[own_rows, :] = chosen.astype(bf16)

    def down_copy(ref, send, recv, source, target):
        at = pl.ds(pl.multiple_of(source * n_pcol, n_pcol), n_pcol)
        return pltpu.make_async_remote_copy(
            src_ref=ref.at[at], dst_ref=ref.at[at],
            send_sem=send.at[target], recv_sem=recv.at[source],
            device_id={"prow": target}, device_id_type=MESH,
        )

    g_copy = functools.partial(down_copy, g_out, g_send, g_recv)
    c_copy = functools.partial(down_copy, c_out, c_send, c_recv)

    @pl.loop(1, n_pcol)
    def _(step):
        s1_copy(lax.rem(pcol + step, n_pcol), pcol).wait_recv()

    g_out[own_rows, :] = rows_buf[:, 0, :].astype(bf16)

    @pl.loop(1, n_prow)
    def _(step):
        g_copy(prow, lax.rem(prow + step, n_prow)).start()

    @pl.loop(1, n_prow)
    def _(step):
        c_copy(prow, lax.rem(prow + step, n_prow)).start()

    @pl.loop(1, n_z)
    def _(step):
        from_z = z_at(step)
        z_copy(from_z, z).wait_recv()
        x_copy(from_z, place).start()

    sib_copy(0, place).start()
    other = (1 - x_hi) * 2 + core

    @pl.loop(0, n_z)
    def _(step):
        x_copy(z_at(step), other).wait_recv()

    sib_copy(1, other).start()

    @pl.loop(1, n_prow)
    def _(step):
        g_copy(lax.rem(prow + step, n_prow), prow).wait_recv()

    @pl.loop(1, n_prow)
    def _(step):
        c_copy(lax.rem(prow + step, n_prow), prow).wait_recv()

    sib_copy(0, x_hi * 2 + 1 - core).wait_recv()
    sib_copy(1, (1 - x_hi) * 2 + 1 - core).wait_recv()

    @pl.loop(1, n_pcol)
    def _(step):
        s1_copy(pcol, lax.rem(pcol + step, n_pcol)).wait_send()

    @pl.loop(1, n_z)
    def _(step):
        z_copy(z, z_at(step)).wait_send()

    @pl.loop(0, n_z)
    def _(step):
        x_copy(z_at(step), place).wait_send()

    sib_copy(0, place).wait_send()
    sib_copy(1, other).wait_send()

    @pl.loop(1, n_prow)
    def _(step):
        g_copy(prow, lax.rem(prow + step, n_prow)).wait_send()
        c_copy(prow, lax.rem(prow + step, n_prow)).wait_send()


def gather_all(n_prow, n_pcol, pivots, panels, trailing):
    rows_dev, width = panels.shape
    n_dev, n_z = n_prow * n_pcol, n_pcol // 4
    dma = pltpu.SemaphoreType.DMA
    vmem = pl.BlockSpec(memory_space=pltpu.VMEM)
    return pl.pallas_call(
        functools.partial(gather_kernel, n_prow, n_pcol),
        out_shape=[
            jax.ShapeDtypeStruct((n_dev, width), bf16),
            jax.ShapeDtypeStruct((n_dev, trailing.shape[1]), bf16),
            jax.ShapeDtypeStruct((n_z, 4, rows_dev, width), bf16),
        ],
        in_specs=[vmem, vmem, pl.BlockSpec(memory_space=pl.ANY)],
        out_specs=[vmem] * 3,
        scratch_shapes=[
            pltpu.VMEM(trailing.shape, bf16),
            pltpu.VMEM((n_pcol, 1, width), f32),
            dma((T_PARTS,)),
            dma((n_pcol,)), dma((n_pcol,)),
            dma((n_z,)), dma((n_z,)), dma((n_z,)), dma((n_z,)),
            dma((2,)), dma((2,)),
            dma((n_prow,)), dma((n_prow,)), dma((n_prow,)), dma((n_prow,)),
        ],
        compiler_params=pltpu.CompilerParams(
            collective_id=0, has_side_effects=True, vmem_limit_bytes=32 * 1024 * 1024
        ),
        name="gather_rows",
    )(pivots, panels, trailing)


def block_elimination(rows, first, extent):
    sub = lax.broadcasted_iota(i32, (extent, 128), 0)
    piece, lane = divmod(first, 128)

    def across(x, k):
        return jnp.broadcast_to(x[k:k + 1, :], (extent, 128))

    columns = [
        jnp.broadcast_to(rows[piece][:, lane + k:lane + k + 1], (extent, 128))
        for k in range(extent)
    ]
    upper = []
    inverse = jnp.zeros((extent, 128), f32)
    for k in range(extent):
        reciprocal = 1.0 / across(columns[k], k)
        factor = jnp.where(sub == k, 0.0, columns[k] * reciprocal)
        inverse = jnp.where(sub == k, reciprocal, inverse)
        upper.append([x[k:k + 1, :] for x in rows[2:]])
        for later in range(k + 1, extent):
            columns[later] = columns[later] - factor * across(columns[later], k)
        rows = [x - factor * across(x, k) for x in rows]
    return [x * inverse for x in rows], upper


def eliminate(work, rhs, lower_inv, extent):
    rhs[...] = jnp.zeros_like(rhs)
    for first in range(0, 256, extent):
        piece, lane = divmod(first, 128)
        block = slice(first, first + extent)
        rows = [work[block, 128 * q:128 * q + 128] for q in range(4)]
        rows, upper = block_elimination(rows, first, extent)
        for k in range(extent):
            for q in range(2):
                lower_inv[first + k:first + k + 1, 128 * q:128 * q + 128] = upper[k][q]
        high, low = split(work[:, 128 * piece:128 * piece + 128])
        left = jnp.concatenate([high, low], axis=1)
        live = [q for q in range(4) if (q + 1) * 128 > first]
        at = (slice(lane, lane + extent), slice(128 + lane, 128 + lane + extent))
        for q in live:
            for part, value in enumerate(split(rows[q])):
                for place in at:
                    rhs[part, place, 128 * q:128 * q + 128] = value
        for half in range(2):
            if half == 0 and first + extent >= 256:
                continue
            columns = slice(256 * half, 256 * half + 256)
            work[:, columns] = work[:, columns] - (
                jnp.dot(left, rhs[0, :, columns], preferred_element_type=f32)
                + jnp.dot(left, rhs[1, :, columns], preferred_element_type=f32)
            )
        for q in live:
            work[block, 128 * q:128 * q + 128] = rows[q]
            for part in range(2):
                for place in at:
                    rhs[part, place, 128 * q:128 * q + 128] = jnp.zeros((extent, 128), bf16)


def solve_kernel(
    rows_dev, pivots, gathered, chosen, panels, trailing, updated, upper_rows,
    work, rhs, lower_inv, t_buf, p_buf, c_buf, x_buf, t_sem, o_sem, p_sem, c_sem,
):
    part_rows = trailing.shape[0] // OUT_PARTS

    def t_copy(q):
        at = pl.ds(q * part_rows, part_rows)
        return pltpu.make_async_copy(trailing.at[at], t_buf.at[at], t_sem.at[q])

    def o_copy(q):
        at = pl.ds(q * part_rows, part_rows)
        return pltpu.make_async_copy(t_buf.at[at], updated.at[at], o_sem.at[q])

    c_copy = pltpu.make_async_copy(chosen, c_buf, c_sem)
    p_copy = pltpu.make_async_copy(panels, p_buf, p_sem)
    c_copy.start()
    p_copy.start()
    for q in range(OUT_PARTS):
        t_copy(q).start()

    block = (pivots[...] // rows_dev).astype(f32)
    for half in range(2):
        turned = jnp.transpose(jnp.broadcast_to(block[half:half + 1, :], (128, 128)))
        for q in range(2):
            lane = lax.broadcasted_iota(i32, (128, 128), 1).astype(f32) + 128 * q
            work[128 * half:128 * half + 128, 256 + 128 * q:384 + 128 * q] = jnp.where(
                turned == lane, 1.0, 0.0
            )
    work[:, :256] = jnp.dot(
        work[:, 256:].astype(bf16), gathered[...], preferred_element_type=f32
    )
    eliminate(work, rhs, lower_inv, 16)

    def product(left, right):
        high, low = split(left)
        return jnp.dot(high, right, preferred_element_type=f32) + jnp.dot(
            low, right, preferred_element_type=f32
        )

    c_copy.wait()
    x_buf[...] = product(work[:, 256:], c_buf[...]).astype(bf16)
    upper_rows[...] = product(lower_inv[...], c_buf[...]).astype(bf16)
    p_copy.wait()
    for q in range(OUT_PARTS):
        t_copy(q).wait()
        at = slice(q * part_rows, (q + 1) * part_rows)
        t_buf[at, :] = (
            t_buf[at, :].astype(f32)
            - jnp.dot(p_buf[at, :], x_buf[...], preferred_element_type=f32)
        ).astype(bf16)
        o_copy(q).start()
    for q in range(OUT_PARTS):
        o_copy(q).wait()


def solve(pivots, gathered, chosen, panels, trailing, rows_dev):
    width, columns = chosen.shape
    dma = pltpu.SemaphoreType.DMA
    vmem, anywhere = pl.BlockSpec(memory_space=pltpu.VMEM), pl.BlockSpec(memory_space=pl.ANY)
    return pl.pallas_call(
        functools.partial(solve_kernel, rows_dev),
        out_shape=[
            jax.ShapeDtypeStruct(trailing.shape, bf16),
            jax.ShapeDtypeStruct((width, columns), bf16),
        ],
        in_specs=[vmem, vmem, anywhere, anywhere, anywhere],
        out_specs=[anywhere, vmem],
        scratch_shapes=[
            pltpu.VMEM((width, 2 * width), f32),
            pltpu.VMEM((2, width, 2 * width), bf16),
            pltpu.VMEM((width, width), f32),
            pltpu.VMEM(trailing.shape, bf16),
            pltpu.VMEM(panels.shape, bf16),
            pltpu.VMEM((width, columns), bf16),
            pltpu.VMEM((width, columns), bf16),
            dma((OUT_PARTS,)), dma((OUT_PARTS,)), dma(()), dma(()),
        ],
        compiler_params=pltpu.CompilerParams(vmem_limit_bytes=40 * 1024 * 1024),
        name="solve_update",
    )(pivots, gathered, chosen, panels, trailing)


def solution(mesh):
    n_prow, n_pcol = mesh.shape["prow"], mesh.shape["pcol"]

    def local(panels, pivots, trailing):
        gathered, chosen, rows = gather_all(n_prow, n_pcol, pivots, panels, trailing)
        rows = rows.reshape(trailing.shape[0], panels.shape[1])
        updated, upper_rows = solve(pivots, gathered, chosen, rows, trailing, panels.shape[0])
        return updated, upper_rows

    return jax.shard_map(
        local,
        mesh=mesh,
        in_specs=(P(("prow", "pcol"), None), P(), P("prow", "pcol")),
        out_specs=(P("prow", "pcol"), P(None, "pcol")),
        check_vma=False,
    )
```

```python
import functools

import jax
import jax.numpy as jnp
from jax import lax
from jax.experimental import pallas as pl
from jax.experimental.pallas import tpu as pltpu
from jax.sharding import PartitionSpec as P

f32, bf16, i32 = jnp.float32, jnp.bfloat16, jnp.int32
MESH = pl.DeviceIdType.MESH
T_PARTS = 4
OUT_PARTS = 8


def split(x):
    high = x.astype(bf16)
    return high, (x - high.astype(f32)).astype(bf16)


def factor_kernel(
    n_prow, n_pcol, pivots, panels, trailing, lower_inv, full_inv, c_out, p_out,
    t_buf, piv_buf, z_rows, q_rows, y_rows, work, order, rhs,
    t_sem, in_sem, a_send, a_recv, z_send, z_recv, x_send, x_recv, sib_send, sib_recv,
    c_send, c_recv,
):
    n_z, n_y = n_pcol // 4, n_prow // 2
    prow, pcol = lax.axis_index("prow"), lax.axis_index("pcol")
    x_lo, y = prow // n_y, lax.rem(prow, n_y)
    z, place = pcol // 4, lax.rem(pcol, 4)
    x_hi, core = place // 2, lax.rem(place, 2)
    q = x_lo * 4 + place
    rows_dev = panels.shape[0]
    part_rows = trailing.shape[0] // T_PARTS

    def t_copy(part):
        at = pl.ds(part * part_rows, part_rows)
        return pltpu.make_async_copy(trailing.at[at], t_buf.at[at], t_sem.at[part])

    piv_copy = pltpu.make_async_copy(pivots, piv_buf, in_sem.at[0])
    own_copy = pltpu.make_async_copy(panels, p_out.at[z, place], in_sem.at[1])
    piv_copy.start()
    own_copy.start()
    for part in range(T_PARTS):
        t_copy(part).start()

    def z_peer(step):
        at = lax.rem(z + step, n_z)
        return at, {"prow": prow, "pcol": at * 4 + place}

    def q_peer(step):
        at = lax.rem(q + step, 8)
        return at, {"prow": (at // 4) * n_y + y, "pcol": z * 4 + lax.rem(at, 4)}

    def y_peer(step):
        at = lax.rem(y + step, n_y)
        return at, {"prow": x_lo * n_y + at, "pcol": pcol}

    groups = ((z_peer, n_z), (q_peer, 8), (y_peer, n_y))
    barrier = pltpu.get_barrier_semaphore()
    for peer, count in groups:
        for step in range(1, count):
            pl.semaphore_signal(barrier, inc=1, device_id=peer(step)[1], device_id_type=MESH)

    piv_copy.wait()
    pivot = piv_buf[...]
    block = pivot // rows_dev
    offset = (pivot - block * rows_dev).astype(f32)
    own = jnp.where(block == prow * n_pcol + pcol, offset, 0.0)
    own_offset = jnp.sum(jnp.sum(own, axis=0, keepdims=True), axis=1, keepdims=True)
    lane = lax.broadcasted_iota(i32, (16, rows_dev), 1).astype(f32)
    pick = jnp.where(lane == own_offset, 1.0, 0.0).astype(bf16)
    own_copy.wait()
    own_row = jnp.dot(pick, p_out[z, place], preferred_element_type=f32)
    z_rows[z] = own_row[0:1, :]
    at_prow, at_pcol = block // n_pcol, lax.rem(block, n_pcol)
    at_q = (at_prow // n_y) * 4 + lax.rem(at_pcol, 4)
    a_at = (lax.rem(at_prow, n_y) * 8 + at_q) * n_z + at_pcol // 4
    for half in range(2):
        for target, where_from in ((work, block), (order, a_at)):
            value = where_from[half:half + 1, :].astype(f32)
            turned = jnp.transpose(jnp.broadcast_to(value, (128, 128)))
            for part in range(2):
                lane = lax.broadcasted_iota(i32, (128, 128), 1).astype(f32) + 128 * part
                first = 256 + 128 * part if target is work else 128 * part
                target[128 * half:128 * half + 128, first:first + 128] = jnp.where(
                    turned == lane, 1.0, 0.0
                ).astype(target.dtype)
    sub = lax.broadcasted_iota(i32, (n_pcol, 128), 0) + prow * n_pcol
    found = jnp.where(block[0:1, :] == sub, offset[0:1, :], 0.0) + jnp.where(
        block[1:2, :] == sub, offset[1:2, :], 0.0
    )
    row_at = jnp.sum(found, axis=1, keepdims=True) + (
        lax.broadcasted_iota(i32, (n_pcol, 1), 0) * rows_dev
    ).astype(f32)
    chosen = jnp.zeros((n_pcol, trailing.shape[1]), f32)
    for part in range(T_PARTS):
        t_copy(part).wait()
        lane = lax.broadcasted_iota(i32, (n_pcol, part_rows), 1).astype(f32) + part * part_rows
        pick = jnp.where(lane == row_at, 1.0, 0.0).astype(bf16)
        chosen = chosen + jnp.dot(
            pick, t_buf[part * part_rows:(part + 1) * part_rows, :], preferred_element_type=f32
        )
    c_out[x_lo, y] = chosen.astype(bf16)

    pl.semaphore_wait(barrier, n_z - 1 + 7 + n_y - 1)

    def a_copy(stage, ref, slot, target):
        return pltpu.make_async_remote_copy(
            src_ref=ref.at[slot], dst_ref=ref.at[slot],
            send_sem=a_send.at[stage], recv_sem=a_recv.at[stage],
            device_id=target, device_id_type=MESH,
        )

    def a_start(stage, ref, slot):
        peer, count = groups[stage]
        for step in range(1, count):
            a_copy(stage, ref, slot, peer(step)[1]).start()

    def a_all(stage, ref):
        return a_copy(stage, ref, pl.ds(0, groups[stage][1] - 1), groups[stage][0](1)[1])

    def z_copy(slot, target):
        return pltpu.make_async_remote_copy(
            src_ref=p_out.at[slot, place], dst_ref=p_out.at[slot, place],
            send_sem=z_send.at[target], recv_sem=z_recv.at[slot],
            device_id={"prow": prow, "pcol": target * 4 + place}, device_id_type=MESH,
        )

    def x_copy(slot, at_place):
        return pltpu.make_async_remote_copy(
            src_ref=p_out.at[slot, at_place], dst_ref=p_out.at[slot, at_place],
            send_sem=x_send.at[slot], recv_sem=x_recv.at[slot],
            device_id={"prow": prow, "pcol": z * 4 + (1 - x_hi) * 2 + core},
            device_id_type=MESH,
        )

    def sib_copy(slot, at_place):
        return pltpu.make_async_remote_copy(
            src_ref=p_out.at[:, at_place], dst_ref=p_out.at[:, at_place],
            send_sem=sib_send.at[slot], recv_sem=sib_recv.at[slot],
            device_id={"prow": prow, "pcol": z * 4 + x_hi * 2 + (1 - core)},
            device_id_type=MESH,
        )

    def c_copy(at_x, at_y, number, slot, target):
        return pltpu.make_async_remote_copy(
            src_ref=c_out.at[at_x, at_y], dst_ref=c_out.at[at_x, at_y],
            send_sem=c_send.at[number], recv_sem=c_recv.at[slot],
            device_id=target, device_id_type=MESH,
        )

    x_other = {"prow": (1 - x_lo) * n_y + y, "pcol": pcol}

    def c_x_copy(at_x):
        return c_copy(at_x, y, 0, 0, x_other)

    def c_y_copy(at_x, at_y, number, step):
        return c_copy(
            at_x, at_y, 1 + number * n_y + step, 1 + number * n_y + at_y, y_peer(step)[1]
        )

    a_start(0, z_rows, z)
    a_all(0, z_rows).wait_recv()
    q_rows[q] = z_rows[:, 0, :]
    a_start(1, q_rows, q)
    near = [1, n_z - 1, 2, n_z - 2, 3, n_z - 3, 4][: n_z - 1]
    for step in near:
        z_copy(z, lax.rem(z + step, n_z)).start()
    a_all(1, q_rows).wait_recv()
    y_rows[y] = q_rows[...].reshape(8 * n_z, 256).astype(bf16)
    a_start(2, y_rows, y)
    c_x_copy(x_lo).start()
    x_copy(z, place).start()
    a_all(2, y_rows).wait_recv()
    work[:, :256] = jnp.dot(
        order[...], y_rows[...].reshape(256, 256), preferred_element_type=f32
    )
    for step in range(1, n_y):
        c_y_copy(x_lo, y, 0, step).start()

    def pass_on(step):
        slot = lax.rem(z + n_z - step, n_z)
        z_copy(slot, z).wait_recv()
        x_copy(slot, place).start()

    def pass_chosen():
        c_x_copy(1 - x_lo).wait_recv()
        for step in range(1, n_y):
            c_y_copy(1 - x_lo, y, 1, step).start()

    other = (1 - x_hi) * 2 + core
    hooks = {
        1: [pass_chosen],
        2: [lambda: pass_on(near[0]), lambda: pass_on(near[1])],
        3: [lambda: pass_on(near[2]), lambda: pass_on(near[3])],
        4: [lambda: pass_on(near[4]), lambda: pass_on(near[5])],
        5: [lambda: pass_on(near[6])],
        6: [lambda: sib_copy(0, place).start()],
    }
    eliminate(work, rhs, lower_inv, 16, hooks)
    full_inv[...] = work[:, 256:]

    for slot in range(n_z):
        x_copy(slot, other).wait_recv()
    sib_copy(1, other).start()
    for step in range(1, n_y):
        at = lax.rem(y + n_y - step, n_y)
        c_y_copy(x_lo, at, 0, step).wait_recv()
        c_y_copy(1 - x_lo, at, 1, step).wait_recv()
    sib_copy(0, x_hi * 2 + 1 - core).wait_recv()
    sib_copy(1, (1 - x_hi) * 2 + 1 - core).wait_recv()

    for stage, ref in enumerate((z_rows, q_rows, y_rows)):
        a_all(stage, ref).wait_send()
    for step in near:
        z_copy(z, lax.rem(z + step, n_z)).wait_send()
    for slot in range(n_z):
        x_copy(slot, place).wait_send()
    sib_copy(0, place).wait_send()
    sib_copy(1, other).wait_send()
    c_x_copy(x_lo).wait_send()
    for step in range(1, n_y):
        c_y_copy(x_lo, y, 0, step).wait_send()
        c_y_copy(1 - x_lo, y, 1, step).wait_send()


def factor(n_prow, n_pcol, pivots, panels, trailing):
    rows_dev, width = panels.shape
    n_z, n_y = n_pcol // 4, n_prow // 2
    columns = trailing.shape[1]
    dma = pltpu.SemaphoreType.DMA
    vmem, hbm = pl.BlockSpec(memory_space=pltpu.VMEM), pl.BlockSpec(memory_space=pltpu.HBM)
    pivots, panels, trailing = (
        pltpu.with_memory_space_constraint(x, pltpu.HBM) for x in (pivots, panels, trailing)
    )
    return pl.pallas_call(
        functools.partial(factor_kernel, n_prow, n_pcol),
        out_shape=[
            jax.ShapeDtypeStruct((width, width), f32),
            jax.ShapeDtypeStruct((width, width), f32),
            jax.ShapeDtypeStruct((2, n_y, n_pcol, columns), bf16),
            jax.ShapeDtypeStruct((n_z, 4, rows_dev, width), bf16),
        ],
        in_specs=[hbm] * 3,
        out_specs=[vmem] * 4,
        scratch_shapes=[
            pltpu.VMEM(trailing.shape, bf16),
            pltpu.VMEM(pivots.shape, i32),
            pltpu.VMEM((n_z, 1, width), f32),
            pltpu.VMEM((8, n_z, width), f32),
            pltpu.VMEM((n_y, 8 * n_z, width), bf16),
            pltpu.VMEM((width, 2 * width), f32),
            pltpu.VMEM((width, width), bf16),
            pltpu.VMEM((2, width, 2 * width), bf16),
            dma((T_PARTS,)), dma((2,)),
            dma((3,)), dma((3,)),
            dma((n_z,)), dma((n_z,)), dma((n_z,)), dma((n_z,)),
            dma((2,)), dma((2,)),
            dma((1 + 2 * n_y,)), dma((1 + 2 * n_y,)),
        ],
        compiler_params=pltpu.CompilerParams(
            collective_id=0, has_side_effects=True, vmem_limit_bytes=32 * 1024 * 1024
        ),
        name="factor_rows",
    )(pivots, panels, trailing)


def block_elimination(rows, first, extent):
    sub = lax.broadcasted_iota(i32, (extent, 128), 0)
    piece, lane = divmod(first, 128)

    def across(x, k):
        return jnp.broadcast_to(x[k:k + 1, :], (extent, 128))

    columns = [
        jnp.broadcast_to(rows[piece][:, lane + k:lane + k + 1], (extent, 128))
        for k in range(extent)
    ]
    upper = []
    inverse = jnp.zeros((extent, 128), f32)
    for k in range(extent):
        reciprocal = 1.0 / across(columns[k], k)
        factor = jnp.where(sub == k, 0.0, columns[k] * reciprocal)
        inverse = jnp.where(sub == k, reciprocal, inverse)
        upper.append([x[k:k + 1, :] for x in rows[2:]])
        for later in range(k + 1, extent):
            columns[later] = columns[later] - factor * across(columns[later], k)
        rows = [x - factor * across(x, k) for x in rows]
    return [x * inverse for x in rows], upper


def eliminate(work, rhs, lower_inv, extent, hooks):
    rhs[...] = jnp.zeros_like(rhs)
    for first in range(0, 256, extent):
        piece, lane = divmod(first, 128)
        block = slice(first, first + extent)
        rows = [work[block, 128 * q:128 * q + 128] for q in range(4)]
        for hook in hooks.get(first // extent, []):
            hook()
        rows, upper = block_elimination(rows, first, extent)
        for k in range(extent):
            for q in range(2):
                lower_inv[first + k:first + k + 1, 128 * q:128 * q + 128] = upper[k][q]
        high, low = split(work[:, 128 * piece:128 * piece + 128])
        left = jnp.concatenate([high, low], axis=1)
        live = [q for q in range(4) if (q + 1) * 128 > first]
        at = (slice(lane, lane + extent), slice(128 + lane, 128 + lane + extent))
        for q in live:
            for part, value in enumerate(split(rows[q])):
                for place in at:
                    rhs[part, place, 128 * q:128 * q + 128] = value
        for half in range(2):
            if half == 0 and first + extent >= 256:
                continue
            columns = slice(256 * half, 256 * half + 256)
            work[:, columns] = work[:, columns] - (
                jnp.dot(left, rhs[0, :, columns], preferred_element_type=f32)
                + jnp.dot(left, rhs[1, :, columns], preferred_element_type=f32)
            )
        for q in live:
            work[block, 128 * q:128 * q + 128] = rows[q]
            for part in range(2):
                for place in at:
                    rhs[part, place, 128 * q:128 * q + 128] = jnp.zeros((extent, 128), bf16)


def solve_kernel(
    lower_inv, full_inv, chosen, panels, trailing, updated, upper_rows, x_buf, o_buf, o_sem
):
    part_rows = trailing.shape[0] // OUT_PARTS

    def o_copy(part):
        at = pl.ds(part * part_rows, part_rows)
        return pltpu.make_async_copy(o_buf.at[at], updated.at[at], o_sem.at[part])

    def product(left, right):
        high, low = split(left)
        return jnp.dot(high, right, preferred_element_type=f32) + jnp.dot(
            low, right, preferred_element_type=f32
        )

    x_buf[...] = product(full_inv[...], chosen[...]).astype(bf16)
    for part in range(OUT_PARTS):
        at = slice(part * part_rows, (part + 1) * part_rows)
        o_buf[at, :] = (
            trailing[at, :].astype(f32)
            - jnp.dot(panels[at, :], x_buf[...], preferred_element_type=f32)
        ).astype(bf16)
        o_copy(part).start()
    upper_rows[...] = product(lower_inv[...], chosen[...]).astype(bf16)
    for part in range(OUT_PARTS):
        o_copy(part).wait()


def solve(lower_inv, full_inv, chosen, panels, trailing):
    width, columns = chosen.shape
    vmem = pl.BlockSpec(memory_space=pltpu.VMEM)
    return pl.pallas_call(
        solve_kernel,
        out_shape=[
            jax.ShapeDtypeStruct(trailing.shape, bf16),
            jax.ShapeDtypeStruct((width, columns), bf16),
        ],
        in_specs=[vmem] * 5,
        out_specs=[pl.BlockSpec(memory_space=pl.ANY), vmem],
        scratch_shapes=[
            pltpu.VMEM((width, columns), bf16),
            pltpu.VMEM(trailing.shape, bf16),
            pltpu.SemaphoreType.DMA((OUT_PARTS,)),
        ],
        compiler_params=pltpu.CompilerParams(vmem_limit_bytes=32 * 1024 * 1024),
        name="solve_update",
    )(lower_inv, full_inv, chosen, panels, trailing)


def solution(mesh):
    n_prow, n_pcol = mesh.shape["prow"], mesh.shape["pcol"]

    def local(panels, pivots, trailing):
        lower_inv, full_inv, chosen, rows = factor(n_prow, n_pcol, pivots, panels, trailing)
        width = panels.shape[1]
        updated, upper_rows = solve(
            lower_inv, full_inv, chosen.reshape(width, trailing.shape[1]),
            rows.reshape(trailing.shape[0], width), trailing,
        )
        return updated, upper_rows

    return jax.shard_map(
        local,
        mesh=mesh,
        in_specs=(P(("prow", "pcol"), None), P(), P("prow", "pcol")),
        out_specs=(P("prow", "pcol"), P(None, "pcol")),
        check_vma=False,
    )
```

```python
import functools

import jax
import jax.numpy as jnp
from jax import lax
from jax.experimental import pallas as pl
from jax.experimental.pallas import tpu as pltpu
from jax.sharding import PartitionSpec as P

f32, bf16, i32 = jnp.float32, jnp.bfloat16, jnp.int32
MESH = pl.DeviceIdType.MESH
T_PARTS = 4
OUT_PARTS = 8


def split(x):
    high = x.astype(bf16)
    return high, (x - high.astype(f32)).astype(bf16)


def factor_kernel(
    n_prow, n_pcol, pivots, panels, trailing, lower_inv, full_inv, c_out, p_out,
    t_buf, piv_buf, g_rows, h_rows, work, order,
    t_sem, in_sem, a_send, a_recv, z_send, z_recv, x_send, x_recv, sib_send, sib_recv,
    c_send, c_recv,
):
    n_z, n_y = n_pcol // 4, n_prow // 2
    prow, pcol = lax.axis_index("prow"), lax.axis_index("pcol")
    x_lo, y = prow // n_y, lax.rem(prow, n_y)
    z, place = pcol // 4, lax.rem(pcol, 4)
    x_hi, core = place // 2, lax.rem(place, 2)
    g, h = z * 2 + core, (x_lo * 2 + x_hi) * n_y + y
    rows_dev = panels.shape[0]
    part_rows = trailing.shape[0] // T_PARTS

    def t_copy(part):
        at = pl.ds(part * part_rows, part_rows)
        return pltpu.make_async_copy(trailing.at[at], t_buf.at[at], t_sem.at[part])

    piv_copy = pltpu.make_async_copy(pivots, piv_buf, in_sem.at[0])
    own_copy = pltpu.make_async_copy(panels, p_out.at[z, place], in_sem.at[1])
    piv_copy.start()
    own_copy.start()
    for part in range(T_PARTS):
        t_copy(part).start()

    def g_peer(step):
        at = lax.rem(g + step, 2 * n_z)
        return {"prow": prow, "pcol": (at // 2) * 4 + x_hi * 2 + lax.rem(at, 2)}

    def h_peer(step):
        at = lax.rem(h + step, 4 * n_y)
        at_x = at // n_y
        return {
            "prow": (at_x // 2) * n_y + lax.rem(at, n_y),
            "pcol": z * 4 + lax.rem(at_x, 2) * 2 + core,
        }

    def y_peer(step):
        return {"prow": x_lo * n_y + lax.rem(y + step, n_y), "pcol": pcol}

    groups = ((g_peer, 2 * n_z), (h_peer, 4 * n_y))
    barrier = pltpu.get_barrier_semaphore()
    for peer, count in groups:
        for step in range(1, count):
            pl.semaphore_signal(barrier, inc=1, device_id=peer(step), device_id_type=MESH)

    piv_copy.wait()
    pivot = piv_buf[...]
    block = pivot // rows_dev
    offset = (pivot - block * rows_dev).astype(f32)
    own = jnp.where(block == prow * n_pcol + pcol, offset, 0.0)
    own_offset = jnp.sum(jnp.sum(own, axis=0, keepdims=True), axis=1, keepdims=True)
    lane = lax.broadcasted_iota(i32, (16, rows_dev), 1).astype(f32)
    pick = jnp.where(lane == own_offset, 1.0, 0.0).astype(bf16)
    own_copy.wait()
    own_row = jnp.dot(pick, p_out[z, place], preferred_element_type=f32)
    g_rows[g] = own_row[0:1, :]
    pl.semaphore_wait(barrier, 2 * n_z - 1 + 4 * n_y - 1)

    def a_copy(stage, ref, slot, target):
        return pltpu.make_async_remote_copy(
            src_ref=ref.at[slot], dst_ref=ref.at[slot],
            send_sem=a_send.at[stage], recv_sem=a_recv.at[stage],
            device_id=target, device_id_type=MESH,
        )

    def a_start(stage, ref, slot):
        peer, count = groups[stage]
        for step in range(1, count):
            a_copy(stage, ref, slot, peer(step)).start()

    def a_all(stage, ref):
        return a_copy(stage, ref, pl.ds(0, groups[stage][1] - 1), groups[stage][0](1))

    def z_copy(slot, target):
        return pltpu.make_async_remote_copy(
            src_ref=p_out.at[slot, place], dst_ref=p_out.at[slot, place],
            send_sem=z_send.at[target], recv_sem=z_recv.at[slot],
            device_id={"prow": prow, "pcol": target * 4 + place}, device_id_type=MESH,
        )

    def x_copy(slot, at_place):
        return pltpu.make_async_remote_copy(
            src_ref=p_out.at[slot, at_place], dst_ref=p_out.at[slot, at_place],
            send_sem=x_send.at[slot], recv_sem=x_recv.at[slot],
            device_id={"prow": prow, "pcol": z * 4 + (1 - x_hi) * 2 + core},
            device_id_type=MESH,
        )

    def sib_copy(slot, at_place):
        return pltpu.make_async_remote_copy(
            src_ref=p_out.at[:, at_place], dst_ref=p_out.at[:, at_place],
            send_sem=sib_send.at[slot], recv_sem=sib_recv.at[slot],
            device_id={"prow": prow, "pcol": z * 4 + x_hi * 2 + (1 - core)},
            device_id_type=MESH,
        )

    def c_copy(at_x, at_y, number, slot, target):
        return pltpu.make_async_remote_copy(
            src_ref=c_out.at[at_x, at_y], dst_ref=c_out.at[at_x, at_y],
            send_sem=c_send.at[number], recv_sem=c_recv.at[slot],
            device_id=target, device_id_type=MESH,
        )

    x_other = {"prow": (1 - x_lo) * n_y + y, "pcol": pcol}

    def c_x_copy(at_x):
        return c_copy(at_x, y, 0, 0, x_other)

    def c_y_copy(at_x, at_y, number, step):
        return c_copy(
            at_x, at_y, 1 + number * n_y + step, 1 + number * n_y + at_y, y_peer(step)
        )

    def pass_on(step):
        slot = lax.rem(z + n_z - step, n_z)
        z_copy(slot, z).wait_recv()
        x_copy(slot, place).start()

    a_start(0, g_rows, g)
    near = [1, n_z - 1, 2, n_z - 2, 3, n_z - 3, 4][: n_z - 1]
    for step in near:
        z_copy(z, lax.rem(z + step, n_z)).start()
    x_copy(z, place).start()
    at_prow, at_pcol = block // n_pcol, lax.rem(block, n_pcol)
    at_x = (at_prow // n_y) * 2 + lax.rem(at_pcol, 4) // 2
    at_h = at_x * n_y + lax.rem(at_prow, n_y)
    a_at = (at_h * n_z + at_pcol // 4) * 2 + lax.rem(at_pcol, 2)
    for half in range(2):
        for target, where_from in ((work, block), (order, a_at)):
            value = where_from[half:half + 1, :].astype(f32)
            turned = jnp.transpose(jnp.broadcast_to(value, (128, 128)))
            for part in range(2):
                lane = lax.broadcasted_iota(i32, (128, 128), 1).astype(f32) + 128 * part
                first = 256 + 128 * part if target is work else 128 * part
                target[128 * half:128 * half + 128, first:first + 128] = jnp.where(
                    turned == lane, 1.0, 0.0
                ).astype(target.dtype)
    a_all(0, g_rows).wait_recv()
    h_rows[h] = g_rows[:, 0, :].astype(bf16)
    a_start(1, h_rows, h)
    sub = lax.broadcasted_iota(i32, (n_pcol, 128), 0) + prow * n_pcol
    found = jnp.where(block[0:1, :] == sub, offset[0:1, :], 0.0) + jnp.where(
        block[1:2, :] == sub, offset[1:2, :], 0.0
    )
    row_at = jnp.sum(found, axis=1, keepdims=True) + (
        lax.broadcasted_iota(i32, (n_pcol, 1), 0) * rows_dev
    ).astype(f32)
    chosen = jnp.zeros((n_pcol, trailing.shape[1]), f32)
    for part in range(T_PARTS):
        t_copy(part).wait()
        lane = lax.broadcasted_iota(i32, (n_pcol, part_rows), 1).astype(f32) + part * part_rows
        pick = jnp.where(lane == row_at, 1.0, 0.0).astype(bf16)
        chosen = chosen + jnp.dot(
            pick, t_buf[part * part_rows:(part + 1) * part_rows, :], preferred_element_type=f32
        )
    c_out[x_lo, y] = chosen.astype(bf16)
    c_x_copy(x_lo).start()
    pass_on(near[0])
    pass_on(near[1])
    a_all(1, h_rows).wait_recv()
    for step in range(1, n_y):
        c_y_copy(x_lo, y, 0, step).start()
    for step in near[2:]:
        pass_on(step)
    sib_copy(0, place).start()
    work[:, :256] = jnp.dot(
        order[...], h_rows[...].reshape(256, 256), preferred_element_type=f32
    )

    def pass_chosen():
        c_x_copy(1 - x_lo).wait_recv()
        for step in range(1, n_y):
            c_y_copy(1 - x_lo, y, 1, step).start()

    other = (1 - x_hi) * 2 + core
    def pass_far():
        for slot in range(n_z):
            x_copy(slot, other).wait_recv()
        sib_copy(1, other).start()

    hooks = {5: [pass_chosen], 9: [pass_far]}
    eliminate(work, lower_inv, 16, hooks)
    full_inv[...] = work[:, 256:]

    for step in range(1, n_y):
        at = lax.rem(y + n_y - step, n_y)
        c_y_copy(x_lo, at, 0, step).wait_recv()
        c_y_copy(1 - x_lo, at, 1, step).wait_recv()
    sib_copy(0, x_hi * 2 + 1 - core).wait_recv()
    sib_copy(1, (1 - x_hi) * 2 + 1 - core).wait_recv()

    for stage, ref in enumerate((g_rows, h_rows)):
        a_all(stage, ref).wait_send()
    for step in near:
        z_copy(z, lax.rem(z + step, n_z)).wait_send()
    for slot in range(n_z):
        x_copy(slot, place).wait_send()
    sib_copy(0, place).wait_send()
    sib_copy(1, other).wait_send()
    c_x_copy(x_lo).wait_send()
    for step in range(1, n_y):
        c_y_copy(x_lo, y, 0, step).wait_send()
        c_y_copy(1 - x_lo, y, 1, step).wait_send()


def factor(n_prow, n_pcol, pivots, panels, trailing):
    rows_dev, width = panels.shape
    n_z, n_y = n_pcol // 4, n_prow // 2
    columns = trailing.shape[1]
    dma = pltpu.SemaphoreType.DMA
    vmem, hbm = pl.BlockSpec(memory_space=pltpu.VMEM), pl.BlockSpec(memory_space=pltpu.HBM)
    pivots, panels, trailing = (
        pltpu.with_memory_space_constraint(x, pltpu.HBM) for x in (pivots, panels, trailing)
    )
    return pl.pallas_call(
        functools.partial(factor_kernel, n_prow, n_pcol),
        out_shape=[
            jax.ShapeDtypeStruct((width, width), f32),
            jax.ShapeDtypeStruct((width, width), f32),
            jax.ShapeDtypeStruct((2, n_y, n_pcol, columns), bf16),
            jax.ShapeDtypeStruct((n_z, 4, rows_dev, width), bf16),
        ],
        in_specs=[hbm] * 3,
        out_specs=[vmem] * 4,
        scratch_shapes=[
            pltpu.VMEM(trailing.shape, bf16),
            pltpu.VMEM(pivots.shape, i32),
            pltpu.VMEM((2 * n_z, 1, width), f32),
            pltpu.VMEM((4 * n_y, 2 * n_z, width), bf16),
            pltpu.VMEM((width, 2 * width), f32),
            pltpu.VMEM((width, width), bf16),
            dma((T_PARTS,)), dma((2,)),
            dma((2,)), dma((2,)),
            dma((n_z,)), dma((n_z,)), dma((n_z,)), dma((n_z,)),
            dma((2,)), dma((2,)),
            dma((1 + 2 * n_y,)), dma((1 + 2 * n_y,)),
        ],
        compiler_params=pltpu.CompilerParams(
            collective_id=0, has_side_effects=True, vmem_limit_bytes=32 * 1024 * 1024
        ),
        name="factor_rows",
    )(pivots, panels, trailing)


def eliminate(work, lower_inv, extent, hooks):
    total = 256
    shape = (extent, 128)
    sub = lax.broadcasted_iota(i32, shape, 0)
    lanes = lax.broadcasted_iota(i32, (total, 128), 1)

    def across(x, k):
        return jnp.broadcast_to(x[k:k + 1, :], shape)

    def column(rows, at):
        piece, lane = divmod(at, 128)
        return jnp.broadcast_to(rows[piece][:, lane:lane + 1], shape)

    def load(first):
        return [work[first:first + extent, 128 * q:128 * q + 128] for q in range(4)]

    rows = load(0)
    for first in range(0, total, extent):
        for hook in hooks.get(first // extent, []):
            hook()
        piece, lane = divmod(first, 128)
        after = first + extent
        last = after >= total
        live = [q for q in range(4) if (q + 1) * 128 > after]
        columns = [column(rows, first + k) for k in range(extent)]
        if not last:
            ahead = load(after)
            ahead_columns = [column(ahead, first + k) for k in range(extent)]
        inverse = jnp.zeros(shape, f32)
        upper = [jnp.zeros(shape, f32)] * 2
        for k in range(extent):
            reciprocal = 1.0 / across(columns[k], k)
            factor = jnp.where(sub == k, 0.0, columns[k] * reciprocal)
            inverse = jnp.where(sub == k, reciprocal, inverse)
            upper = [jnp.where(sub == k, rows[2 + q], upper[q]) for q in range(2)]
            pivot_row = {q: across(rows[q], k) for q in live}
            pivot_columns = [across(columns[j], k) for j in range(k + 1, extent)]
            if not last:
                times = ahead_columns[k] * reciprocal
                for j in range(k + 1, extent):
                    ahead_columns[j] = ahead_columns[j] - times * pivot_columns[j - k - 1]
                for q in live:
                    ahead[q] = ahead[q] - times * pivot_row[q]
            for j in range(k + 1, extent):
                columns[j] = columns[j] - factor * pivot_columns[j - k - 1]
            for q in live:
                rows[q] = rows[q] - factor * pivot_row[q]
        rows = [x * inverse for x in rows]
        for q in range(2):
            lower_inv[first:after, 128 * q:128 * q + 128] = upper[q]
        group = work[:, 128 * piece:128 * piece + 128]
        high = group.astype(bf16).astype(f32)
        low = group - high
        second, third = (lane + extent) % 128, (lane + 2 * extent) % 128
        left = jnp.where(
            (lanes >= lane) & (lanes < lane + extent), high,
            jnp.where((lanes >= second) & (lanes < second + extent), pltpu.roll(low, extent, 1),
                      pltpu.roll(high, 2 * extent, 1)),
        ).astype(bf16)
        blank = jnp.zeros(shape, bf16)
        for pair in [live[:-2], live[-2:]] if len(live) > 2 else [live]:
            tiles = []
            for p in pair:
                xh, xl = split(rows[p])
                parts = [blank] * (128 // extent)
                parts[lane // extent], parts[second // extent], parts[third // extent] = xh, xh, xl
                tiles.append(jnp.concatenate(parts, axis=0))
            right = jnp.concatenate(tiles, axis=1) if len(tiles) > 1 else tiles[0]
            cs = slice(128 * pair[0], 128 * (pair[-1] + 1))
            for lo_row, hi_row in ((0, first), (after + extent, total)):
                if hi_row <= lo_row:
                    continue
                work[lo_row:hi_row, cs] = work[lo_row:hi_row, cs] - jnp.dot(
                    left[lo_row:hi_row], right, preferred_element_type=f32)
        for q in live:
            work[first:after, 128 * q:128 * q + 128] = rows[q]
        if not last:
            rows = ahead

def solve_kernel(
    lower_inv, full_inv, chosen, panels, trailing, updated, upper_rows, x_buf, o_buf, o_sem
):
    part_rows = trailing.shape[0] // OUT_PARTS

    def o_copy(part):
        at = pl.ds(part * part_rows, part_rows)
        return pltpu.make_async_copy(o_buf.at[at], updated.at[at], o_sem.at[part])

    def product(left, right):
        high, low = split(left)
        return jnp.dot(high, right, preferred_element_type=f32) + jnp.dot(
            low, right, preferred_element_type=f32
        )

    x_buf[...] = product(full_inv[...], chosen[...]).astype(bf16)
    for part in range(OUT_PARTS):
        at = slice(part * part_rows, (part + 1) * part_rows)
        o_buf[at, :] = (
            trailing[at, :].astype(f32)
            - jnp.dot(panels[at, :], x_buf[...], preferred_element_type=f32)
        ).astype(bf16)
        o_copy(part).start()
    upper_rows[...] = product(lower_inv[...], chosen[...]).astype(bf16)
    for part in range(OUT_PARTS):
        o_copy(part).wait()


def solve(lower_inv, full_inv, chosen, panels, trailing):
    width, columns = chosen.shape
    vmem = pl.BlockSpec(memory_space=pltpu.VMEM)
    return pl.pallas_call(
        solve_kernel,
        out_shape=[
            jax.ShapeDtypeStruct(trailing.shape, bf16),
            jax.ShapeDtypeStruct((width, columns), bf16),
        ],
        in_specs=[vmem] * 5,
        out_specs=[pl.BlockSpec(memory_space=pl.ANY), vmem],
        scratch_shapes=[
            pltpu.VMEM((width, columns), bf16),
            pltpu.VMEM(trailing.shape, bf16),
            pltpu.SemaphoreType.DMA((OUT_PARTS,)),
        ],
        compiler_params=pltpu.CompilerParams(vmem_limit_bytes=32 * 1024 * 1024),
        name="solve_update",
    )(lower_inv, full_inv, chosen, panels, trailing)


def solution(mesh):
    n_prow, n_pcol = mesh.shape["prow"], mesh.shape["pcol"]

    def local(panels, pivots, trailing):
        lower_inv, full_inv, chosen, rows = factor(n_prow, n_pcol, pivots, panels, trailing)
        width = panels.shape[1]
        updated, upper_rows = solve(
            lower_inv, full_inv, chosen.reshape(width, trailing.shape[1]),
            rows.reshape(trailing.shape[0], width), trailing,
        )
        return updated, upper_rows

    return jax.shard_map(
        local,
        mesh=mesh,
        in_specs=(P(("prow", "pcol"), None), P(), P("prow", "pcol")),
        out_specs=(P("prow", "pcol"), P(None, "pcol")),
        check_vma=False,
    )
```

```python
import functools

import jax
import jax.numpy as jnp
from jax import lax
from jax.experimental import pallas as pl
from jax.experimental.pallas import tpu as pltpu
from jax.sharding import PartitionSpec as P

f32, bf16, i32 = jnp.float32, jnp.bfloat16, jnp.int32
MESH = pl.DeviceIdType.MESH
T_PARTS = 4
OUT_PARTS = 8


def split(x):
    high = x.astype(bf16)
    return high, (x - high.astype(f32)).astype(bf16)


def factor_kernel(
    n_prow, n_pcol, pivots, panels, trailing, lower_inv, full_inv, c_out, p_out,
    t_buf, piv_buf, g_rows, h_rows, work, order,
    t_sem, in_sem, a_send, a_recv, z_send, z_recv, x_send, x_recv, w_send, w_recv, sib_send, sib_recv,
    c_send, c_recv,
):
    n_z, n_y = n_pcol // 4, n_prow // 2
    prow, pcol = lax.axis_index("prow"), lax.axis_index("pcol")
    x_lo, y = prow // n_y, lax.rem(prow, n_y)
    z, place = pcol // 4, lax.rem(pcol, 4)
    x_hi, core = place // 2, lax.rem(place, 2)
    g, h = z * 2 + core, (x_lo * 2 + x_hi) * n_y + y
    other = (1 - x_hi) * 2 + core
    rows_dev = panels.shape[0]
    part_rows = trailing.shape[0] // T_PARTS

    def t_copy(part):
        at = pl.ds(part * part_rows, part_rows)
        return pltpu.make_async_copy(trailing.at[at], t_buf.at[at], t_sem.at[part])

    piv_copy = pltpu.make_async_copy(pivots, piv_buf, in_sem.at[0])
    own_copy = pltpu.make_async_copy(panels, p_out.at[z, place], in_sem.at[1])
    piv_copy.start()
    own_copy.start()
    for part in range(T_PARTS):
        t_copy(part).start()

    def g_peer(step):
        to_z, to_core = step
        at_z, at_core = lax.rem(z + to_z, n_z), lax.rem(core + to_core, 2)
        return {"prow": prow, "pcol": at_z * 4 + x_hi * 2 + at_core}

    def h_peer(step):
        to_hi, to_lo, to_y = step
        at_hi, at_lo = lax.rem(x_hi + to_hi, 2), lax.rem(x_lo + to_lo, 2)
        return {
            "prow": at_lo * n_y + lax.rem(y + to_y, n_y),
            "pcol": z * 4 + at_hi * 2 + core,
        }

    def y_peer(step):
        return {"prow": x_lo * n_y + lax.rem(y + step, n_y), "pcol": pcol}

    def hops(distance, around):
        return min(distance, around - distance)

    g_steps = sorted(
        ((to_z, to_core) for to_z in range(n_z) for to_core in range(2) if to_z + to_core),
        key=lambda step: (-hops(step[0], n_z), step),
    )
    h_steps = sorted(
        ((hi, lo, to_y) for hi in range(2) for lo in range(2) for to_y in range(n_y)
         if hi + lo + to_y),
        key=lambda step: (-hops(step[2], n_y) - (0, 1, 2, 1)[2 * step[0] + step[1]], step),
    )
    groups = ((g_peer, g_steps), (h_peer, h_steps))
    barrier = pltpu.get_barrier_semaphore()
    for peer, steps in groups:
        for step in steps:
            pl.semaphore_signal(barrier, inc=1, device_id=peer(step), device_id_type=MESH)

    piv_copy.wait()
    pivot = piv_buf[...]
    block = pivot // rows_dev
    offset = (pivot - block * rows_dev).astype(f32)
    own = jnp.where(block == prow * n_pcol + pcol, offset, 0.0)
    own_offset = jnp.sum(jnp.sum(own, axis=0, keepdims=True), axis=1, keepdims=True)
    lane = lax.broadcasted_iota(i32, (16, rows_dev), 1).astype(f32)
    pick = jnp.where(lane == own_offset, 1.0, 0.0).astype(bf16)
    own_copy.wait()
    own_row = jnp.dot(pick, p_out[z, place], preferred_element_type=f32)
    g_rows[g] = own_row[0:1, :]
    pl.semaphore_wait(barrier, 2 * n_z - 1 + 4 * n_y - 1)

    def a_copy(stage, ref, slot, target):
        return pltpu.make_async_remote_copy(
            src_ref=ref.at[slot], dst_ref=ref.at[slot],
            send_sem=a_send.at[stage], recv_sem=a_recv.at[stage],
            device_id=target, device_id_type=MESH,
        )

    def a_start(stage, ref, slot):
        peer, steps = groups[stage]
        for step in steps:
            a_copy(stage, ref, slot, peer(step)).start()

    def a_all(stage, ref):
        return a_copy(stage, ref, pl.ds(0, len(groups[stage][1])), y_peer(1))

    def z_copy(slot, target):
        return pltpu.make_async_remote_copy(
            src_ref=p_out.at[slot, place], dst_ref=p_out.at[slot, place],
            send_sem=z_send.at[target], recv_sem=z_recv.at[slot],
            device_id={"prow": prow, "pcol": target * 4 + place}, device_id_type=MESH,
        )

    def x_copy(slot, at_place):
        return pltpu.make_async_remote_copy(
            src_ref=p_out.at[slot, at_place], dst_ref=p_out.at[slot, at_place],
            send_sem=x_send.at[slot], recv_sem=x_recv.at[slot],
            device_id={"prow": prow, "pcol": z * 4 + (1 - x_hi) * 2 + core},
            device_id_type=MESH,
        )

    def w_copy(slot, target):
        return pltpu.make_async_remote_copy(
            src_ref=p_out.at[slot, other], dst_ref=p_out.at[slot, other],
            send_sem=w_send.at[target], recv_sem=w_recv.at[slot],
            device_id={"prow": prow, "pcol": target * 4 + place}, device_id_type=MESH,
        )

    def sib_copy(slot, at_place):
        return pltpu.make_async_remote_copy(
            src_ref=p_out.at[:, at_place], dst_ref=p_out.at[:, at_place],
            send_sem=sib_send.at[slot], recv_sem=sib_recv.at[slot],
            device_id={"prow": prow, "pcol": z * 4 + x_hi * 2 + (1 - core)},
            device_id_type=MESH,
        )

    def c_copy(at_x, at_y, number, slot, target):
        return pltpu.make_async_remote_copy(
            src_ref=c_out.at[at_x, at_y], dst_ref=c_out.at[at_x, at_y],
            send_sem=c_send.at[number], recv_sem=c_recv.at[slot],
            device_id=target, device_id_type=MESH,
        )

    x_other = {"prow": (1 - x_lo) * n_y + y, "pcol": pcol}

    def c_x_copy(at_x):
        return c_copy(at_x, y, 0, 0, x_other)

    def c_y_copy(at_x, at_y, number, step):
        return c_copy(
            at_x, at_y, 1 + number * n_y + step, 1 + number * n_y + at_y, y_peer(step)
        )

    def beside(step):
        return lax.rem(z + step + n_z, n_z)

    a_start(0, g_rows, g)
    near, far = (1, -1, 2, -2), (3, -3, 4)
    for step in far + near:
        z_copy(z, beside(step)).start()
    x_copy(z, place).start()
    at_prow, at_pcol = block // n_pcol, lax.rem(block, n_pcol)
    at_x = (at_prow // n_y) * 2 + lax.rem(at_pcol, 4) // 2
    at_h = at_x * n_y + lax.rem(at_prow, n_y)
    a_at = (at_h * n_z + at_pcol // 4) * 2 + lax.rem(at_pcol, 2)
    for half in range(2):
        for target, where_from in ((work, block), (order, a_at)):
            value = where_from[half:half + 1, :].astype(f32)
            turned = jnp.transpose(jnp.broadcast_to(value, (128, 128)))
            for part in range(2):
                lane = lax.broadcasted_iota(i32, (128, 128), 1).astype(f32) + 128 * part
                first = 256 + 128 * part if target is work else 128 * part
                target[128 * half:128 * half + 128, first:first + 128] = jnp.where(
                    turned == lane, 1.0, 0.0
                ).astype(target.dtype)
    x_copy(z, other).wait_recv()
    for step in near:
        w_copy(z, beside(step)).start()
    a_all(0, g_rows).wait_recv()
    h_rows[h] = g_rows[:, 0, :].astype(bf16)
    a_start(1, h_rows, h)
    sub = lax.broadcasted_iota(i32, (n_pcol, 128), 0) + prow * n_pcol
    found = jnp.where(block[0:1, :] == sub, offset[0:1, :], 0.0) + jnp.where(
        block[1:2, :] == sub, offset[1:2, :], 0.0
    )
    row_at = jnp.sum(found, axis=1, keepdims=True) + (
        lax.broadcasted_iota(i32, (n_pcol, 1), 0) * rows_dev
    ).astype(f32)
    chosen = jnp.zeros((n_pcol, trailing.shape[1]), f32)
    for part in range(T_PARTS):
        t_copy(part).wait()
        lane = lax.broadcasted_iota(i32, (n_pcol, part_rows), 1).astype(f32) + part * part_rows
        pick = jnp.where(lane == row_at, 1.0, 0.0).astype(bf16)
        chosen = chosen + jnp.dot(
            pick, t_buf[part * part_rows:(part + 1) * part_rows, :], preferred_element_type=f32
        )
    c_out[x_lo, y] = chosen.astype(bf16)
    c_x_copy(x_lo).start()
    for step in far:
        z_copy(beside(-step), z).wait_recv()
        x_copy(beside(-step), place).start()
    for step in near:
        z_copy(beside(-step), z).wait_recv()
    sib_copy(0, place).start()
    for step in range(1, n_y):
        c_y_copy(x_lo, y, 0, step).start()
    a_all(1, h_rows).wait_recv()
    work[:, :256] = jnp.dot(
        order[...], h_rows[...].reshape(256, 256), preferred_element_type=f32
    )

    def pass_chosen():
        c_x_copy(1 - x_lo).wait_recv()
        for step in range(1, n_y):
            c_y_copy(1 - x_lo, y, 1, step).start()

    def pass_far():
        for step in near:
            w_copy(beside(-step), z).wait_recv()
        for step in far:
            x_copy(beside(-step), other).wait_recv()
        sib_copy(1, other).start()

    hooks = {4: [pass_chosen], 8: [pass_far]}
    eliminate(work, lower_inv, 16, hooks)
    full_inv[...] = work[:, 256:]

    for step in range(1, n_y):
        at = lax.rem(y + n_y - step, n_y)
        c_y_copy(x_lo, at, 0, step).wait_recv()
        c_y_copy(1 - x_lo, at, 1, step).wait_recv()
    sib_copy(0, x_hi * 2 + 1 - core).wait_recv()
    sib_copy(1, (1 - x_hi) * 2 + 1 - core).wait_recv()

    for stage, ref in enumerate((g_rows, h_rows)):
        a_all(stage, ref).wait_send()
    for step in far + near:
        z_copy(z, beside(step)).wait_send()
    for step in near:
        w_copy(z, beside(step)).wait_send()
    for step in (0,) + far:
        x_copy(beside(-step), place).wait_send()
    sib_copy(0, place).wait_send()
    sib_copy(1, other).wait_send()
    c_x_copy(x_lo).wait_send()
    for step in range(1, n_y):
        c_y_copy(x_lo, y, 0, step).wait_send()
        c_y_copy(1 - x_lo, y, 1, step).wait_send()


def factor(n_prow, n_pcol, pivots, panels, trailing):
    rows_dev, width = panels.shape
    n_z, n_y = n_pcol // 4, n_prow // 2
    columns = trailing.shape[1]
    dma = pltpu.SemaphoreType.DMA
    vmem, hbm = pl.BlockSpec(memory_space=pltpu.VMEM), pl.BlockSpec(memory_space=pltpu.HBM)
    pivots, panels, trailing = (
        pltpu.with_memory_space_constraint(x, pltpu.HBM) for x in (pivots, panels, trailing)
    )
    return pl.pallas_call(
        functools.partial(factor_kernel, n_prow, n_pcol),
        out_shape=[
            jax.ShapeDtypeStruct((width, width), f32),
            jax.ShapeDtypeStruct((width, width), f32),
            jax.ShapeDtypeStruct((2, n_y, n_pcol, columns), bf16),
            jax.ShapeDtypeStruct((n_z, 4, rows_dev, width), bf16),
        ],
        in_specs=[hbm] * 3,
        out_specs=[vmem] * 4,
        scratch_shapes=[
            pltpu.VMEM(trailing.shape, bf16),
            pltpu.VMEM(pivots.shape, i32),
            pltpu.VMEM((2 * n_z, 1, width), f32),
            pltpu.VMEM((4 * n_y, 2 * n_z, width), bf16),
            pltpu.VMEM((width, 2 * width), f32),
            pltpu.VMEM((width, width), bf16),
            dma((T_PARTS,)), dma((2,)),
            dma((2,)), dma((2,)),
            dma((n_z,)), dma((n_z,)), dma((n_z,)), dma((n_z,)), dma((n_z,)), dma((n_z,)),
            dma((2,)), dma((2,)),
            dma((1 + 2 * n_y,)), dma((1 + 2 * n_y,)),
        ],
        compiler_params=pltpu.CompilerParams(
            collective_id=0, has_side_effects=True, vmem_limit_bytes=32 * 1024 * 1024
        ),
        name="factor_rows",
    )(pivots, panels, trailing)


def eliminate(work, lower_inv, extent, hooks):
    total = 256
    shape = (extent, 128)
    sub = lax.broadcasted_iota(i32, shape, 0)
    lanes = lax.broadcasted_iota(i32, (total, 128), 1)

    def across(x, k):
        return jnp.broadcast_to(x[k:k + 1, :], shape)

    def column(rows, at):
        piece, lane = divmod(at, 128)
        return jnp.broadcast_to(rows[piece][:, lane:lane + 1], shape)

    def load(first):
        return [work[first:first + extent, 128 * q:128 * q + 128] for q in range(4)]

    rows = load(0)
    for first in range(0, total, extent):
        for hook in hooks.get(first // extent, []):
            hook()
        piece, lane = divmod(first, 128)
        after = first + extent
        last = after >= total
        live = [q for q in range(4) if (q + 1) * 128 > after]
        columns = [column(rows, first + k) for k in range(extent)]
        if not last:
            ahead = load(after)
            ahead_columns = [column(ahead, first + k) for k in range(extent)]
        inverse = jnp.zeros(shape, f32)
        upper = [jnp.zeros(shape, f32)] * 2
        for k in range(extent):
            reciprocal = 1.0 / across(columns[k], k)
            factor = jnp.where(sub == k, 0.0, columns[k] * reciprocal)
            inverse = jnp.where(sub == k, reciprocal, inverse)
            upper = [jnp.where(sub == k, rows[2 + q], upper[q]) for q in range(2)]
            pivot_row = {q: across(rows[q], k) for q in live}
            pivot_columns = [across(columns[j], k) for j in range(k + 1, extent)]
            if not last:
                times = ahead_columns[k] * reciprocal
                for j in range(k + 1, extent):
                    ahead_columns[j] = ahead_columns[j] - times * pivot_columns[j - k - 1]
                for q in live:
                    ahead[q] = ahead[q] - times * pivot_row[q]
            for j in range(k + 1, extent):
                columns[j] = columns[j] - factor * pivot_columns[j - k - 1]
            for q in live:
                rows[q] = rows[q] - factor * pivot_row[q]
        rows = [x * inverse for x in rows]
        for q in range(2):
            lower_inv[first:after, 128 * q:128 * q + 128] = upper[q]
        group = work[:, 128 * piece:128 * piece + 128]
        high = group.astype(bf16).astype(f32)
        low = group - high
        second, third = (lane + extent) % 128, (lane + 2 * extent) % 128
        left = jnp.where(
            (lanes >= lane) & (lanes < lane + extent), high,
            jnp.where((lanes >= second) & (lanes < second + extent), pltpu.roll(low, extent, 1),
                      pltpu.roll(high, 2 * extent, 1)),
        ).astype(bf16)
        blank = jnp.zeros(shape, bf16)
        for pair in [live[:-2], live[-2:]] if len(live) > 2 else [live]:
            tiles = []
            for p in pair:
                xh, xl = split(rows[p])
                parts = [blank] * (128 // extent)
                parts[lane // extent], parts[second // extent], parts[third // extent] = xh, xh, xl
                tiles.append(jnp.concatenate(parts, axis=0))
            right = jnp.concatenate(tiles, axis=1) if len(tiles) > 1 else tiles[0]
            cs = slice(128 * pair[0], 128 * (pair[-1] + 1))
            for lo_row, hi_row in ((0, first), (after + extent, total)):
                if hi_row <= lo_row:
                    continue
                work[lo_row:hi_row, cs] = work[lo_row:hi_row, cs] - jnp.dot(
                    left[lo_row:hi_row], right, preferred_element_type=f32)
        for q in live:
            work[first:after, 128 * q:128 * q + 128] = rows[q]
        if not last:
            rows = ahead

def solve_kernel(
    lower_inv, full_inv, chosen, panels, trailing, updated, upper_rows, x_buf, o_buf, o_sem
):
    part_rows = trailing.shape[0] // OUT_PARTS

    def o_copy(part):
        at = pl.ds(part * part_rows, part_rows)
        return pltpu.make_async_copy(o_buf.at[at], updated.at[at], o_sem.at[part])

    def product(left, right):
        high, low = split(left)
        return jnp.dot(high, right, preferred_element_type=f32) + jnp.dot(
            low, right, preferred_element_type=f32
        )

    x_buf[...] = product(full_inv[...], chosen[...]).astype(bf16)
    for part in range(OUT_PARTS):
        at = slice(part * part_rows, (part + 1) * part_rows)
        o_buf[at, :] = (
            trailing[at, :].astype(f32)
            - jnp.dot(panels[at, :], x_buf[...], preferred_element_type=f32)
        ).astype(bf16)
        o_copy(part).start()
    upper_rows[...] = product(lower_inv[...], chosen[...]).astype(bf16)
    for part in range(OUT_PARTS):
        o_copy(part).wait()


def solve(lower_inv, full_inv, chosen, panels, trailing):
    width, columns = chosen.shape
    vmem = pl.BlockSpec(memory_space=pltpu.VMEM)
    return pl.pallas_call(
        solve_kernel,
        out_shape=[
            jax.ShapeDtypeStruct(trailing.shape, bf16),
            jax.ShapeDtypeStruct((width, columns), bf16),
        ],
        in_specs=[vmem] * 5,
        out_specs=[pl.BlockSpec(memory_space=pl.ANY), vmem],
        scratch_shapes=[
            pltpu.VMEM((width, columns), bf16),
            pltpu.VMEM(trailing.shape, bf16),
            pltpu.SemaphoreType.DMA((OUT_PARTS,)),
        ],
        compiler_params=pltpu.CompilerParams(vmem_limit_bytes=32 * 1024 * 1024),
        name="solve_update",
    )(lower_inv, full_inv, chosen, panels, trailing)


def solution(mesh):
    n_prow, n_pcol = mesh.shape["prow"], mesh.shape["pcol"]

    def local(panels, pivots, trailing):
        lower_inv, full_inv, chosen, rows = factor(n_prow, n_pcol, pivots, panels, trailing)
        width = panels.shape[1]
        updated, upper_rows = solve(
            lower_inv, full_inv, chosen.reshape(width, trailing.shape[1]),
            rows.reshape(trailing.shape[0], width), trailing,
        )
        return updated, upper_rows

    return jax.shard_map(
        local,
        mesh=mesh,
        in_specs=(P(("prow", "pcol"), None), P(), P("prow", "pcol")),
        out_specs=(P("prow", "pcol"), P(None, "pcol")),
        check_vma=False,
    )
```

```python
import functools

import jax
import jax.numpy as jnp
from jax import lax
from jax.experimental import pallas as pl
from jax.experimental.pallas import tpu as pltpu
from jax.sharding import PartitionSpec as P

f32, bf16, i32 = jnp.float32, jnp.bfloat16, jnp.int32
MESH = pl.DeviceIdType.MESH
T_PARTS = 4
OUT_PARTS = 8


def split(x):
    high = x.astype(bf16)
    return high, (x - high.astype(f32)).astype(bf16)


def factor_kernel(
    n_prow, n_pcol, pivots, panels, trailing, lower_inv, full_inv, c_out, p_out,
    t_buf, piv_buf, g_rows, h_rows, work, order,
    t_sem, in_sem, a_send, a_recv, z_send, z_recv, x_send, x_recv, w_send, w_recv, sib_send, sib_recv,
    c_send, c_recv,
):
    n_z, n_y = n_pcol // 4, n_prow // 2
    prow, pcol = lax.axis_index("prow"), lax.axis_index("pcol")
    x_lo, y = prow // n_y, lax.rem(prow, n_y)
    z, place = pcol // 4, lax.rem(pcol, 4)
    x_hi, core = place // 2, lax.rem(place, 2)
    g, h = z * 2 + core, (x_lo * 2 + x_hi) * n_y + y
    other = (1 - x_hi) * 2 + core
    rows_dev = panels.shape[0]
    part_rows = trailing.shape[0] // T_PARTS

    def t_copy(part):
        at = pl.ds(part * part_rows, part_rows)
        return pltpu.make_async_copy(trailing.at[at], t_buf.at[at], t_sem.at[part])

    piv_copy = pltpu.make_async_copy(pivots, piv_buf, in_sem.at[0])
    own_copy = pltpu.make_async_copy(panels, p_out.at[z, place], in_sem.at[1])
    piv_copy.start()
    own_copy.start()
    for part in range(T_PARTS):
        t_copy(part).start()

    def g_peer(step):
        to_z, to_core = step
        at_z, at_core = lax.rem(z + to_z, n_z), lax.rem(core + to_core, 2)
        return {"prow": prow, "pcol": at_z * 4 + x_hi * 2 + at_core}

    def h_peer(step):
        to_hi, to_lo, to_y = step
        at_hi, at_lo = lax.rem(x_hi + to_hi, 2), lax.rem(x_lo + to_lo, 2)
        return {
            "prow": at_lo * n_y + lax.rem(y + to_y, n_y),
            "pcol": z * 4 + at_hi * 2 + core,
        }

    def y_peer(step):
        return {"prow": x_lo * n_y + lax.rem(y + step, n_y), "pcol": pcol}

    def hops(distance, around):
        return min(distance, around - distance)

    g_steps = sorted(
        ((to_z, to_core) for to_z in range(n_z) for to_core in range(2) if to_z + to_core),
        key=lambda step: (-hops(step[0], n_z), step),
    )
    h_steps = sorted(
        ((hi, lo, to_y) for hi in range(2) for lo in range(2) for to_y in range(n_y)
         if hi + lo + to_y),
        key=lambda step: (-hops(step[2], n_y) - (0, 1, 2, 1)[2 * step[0] + step[1]], step),
    )
    groups = ((g_peer, g_steps), (h_peer, h_steps))
    barrier = pltpu.get_barrier_semaphore()
    for peer, steps in groups:
        for step in steps:
            pl.semaphore_signal(barrier, inc=1, device_id=peer(step), device_id_type=MESH)

    piv_copy.wait()
    pivot = piv_buf[...]
    block = pivot // rows_dev
    offset = (pivot - block * rows_dev).astype(f32)
    own = jnp.where(block == prow * n_pcol + pcol, offset, 0.0)
    own_offset = jnp.sum(jnp.sum(own, axis=0, keepdims=True), axis=1, keepdims=True)
    lane = lax.broadcasted_iota(i32, (16, rows_dev), 1).astype(f32)
    pick = jnp.where(lane == own_offset, 1.0, 0.0).astype(bf16)
    own_copy.wait()
    own_row = jnp.dot(pick, p_out[z, place], preferred_element_type=f32)
    g_rows[g] = own_row[0:1, :]
    pl.semaphore_wait(barrier, 2 * n_z - 1 + 4 * n_y - 1)

    def a_copy(stage, ref, slot, target):
        return pltpu.make_async_remote_copy(
            src_ref=ref.at[slot], dst_ref=ref.at[slot],
            send_sem=a_send.at[stage], recv_sem=a_recv.at[stage],
            device_id=target, device_id_type=MESH,
        )

    def a_start(stage, ref, slot):
        peer, steps = groups[stage]
        for step in steps:
            a_copy(stage, ref, slot, peer(step)).start()

    def a_all(stage, ref):
        return a_copy(stage, ref, pl.ds(0, len(groups[stage][1])), y_peer(1))

    def z_copy(slot, target):
        return pltpu.make_async_remote_copy(
            src_ref=p_out.at[slot, place], dst_ref=p_out.at[slot, place],
            send_sem=z_send.at[target], recv_sem=z_recv.at[slot],
            device_id={"prow": prow, "pcol": target * 4 + place}, device_id_type=MESH,
        )

    def x_copy(slot, at_place):
        return pltpu.make_async_remote_copy(
            src_ref=p_out.at[slot, at_place], dst_ref=p_out.at[slot, at_place],
            send_sem=x_send.at[slot], recv_sem=x_recv.at[slot],
            device_id={"prow": prow, "pcol": z * 4 + (1 - x_hi) * 2 + core},
            device_id_type=MESH,
        )

    def w_copy(slot, target):
        return pltpu.make_async_remote_copy(
            src_ref=p_out.at[slot, other], dst_ref=p_out.at[slot, other],
            send_sem=w_send.at[target], recv_sem=w_recv.at[slot],
            device_id={"prow": prow, "pcol": target * 4 + place}, device_id_type=MESH,
        )

    def sib_copy(slot, at_place):
        return pltpu.make_async_remote_copy(
            src_ref=p_out.at[:, at_place], dst_ref=p_out.at[:, at_place],
            send_sem=sib_send.at[slot], recv_sem=sib_recv.at[slot],
            device_id={"prow": prow, "pcol": z * 4 + x_hi * 2 + (1 - core)},
            device_id_type=MESH,
        )

    def c_copy(at_x, at_y, number, slot, target):
        return pltpu.make_async_remote_copy(
            src_ref=c_out.at[at_x, at_y], dst_ref=c_out.at[at_x, at_y],
            send_sem=c_send.at[number], recv_sem=c_recv.at[slot],
            device_id=target, device_id_type=MESH,
        )

    x_other = {"prow": (1 - x_lo) * n_y + y, "pcol": pcol}

    def c_x_copy(at_x):
        return c_copy(at_x, y, 0, 0, x_other)

    def c_y_copy(at_x, at_y, number, step):
        return c_copy(
            at_x, at_y, 1 + number * n_y + step, 1 + number * n_y + at_y, y_peer(step)
        )

    def beside(step):
        return lax.rem(z + step + n_z, n_z)

    a_start(0, g_rows, g)
    near, far = (1, -1, 2, -2), (3, -3, 4)
    for step in far + near:
        z_copy(z, beside(step)).start()
    x_copy(z, place).start()
    at_prow, at_pcol = block // n_pcol, lax.rem(block, n_pcol)
    at_x = (at_prow // n_y) * 2 + lax.rem(at_pcol, 4) // 2
    at_h = at_x * n_y + lax.rem(at_prow, n_y)
    a_at = (at_h * n_z + at_pcol // 4) * 2 + lax.rem(at_pcol, 2)
    for half in range(2):
        for target, where_from in ((work, block), (order, a_at)):
            value = where_from[half:half + 1, :].astype(f32)
            turned = jnp.transpose(jnp.broadcast_to(value, (128, 128)))
            for part in range(2):
                lane = lax.broadcasted_iota(i32, (128, 128), 1).astype(f32) + 128 * part
                first = 256 + 128 * part if target is work else 128 * part
                target[128 * half:128 * half + 128, first:first + 128] = jnp.where(
                    turned == lane, 1.0, 0.0
                ).astype(target.dtype)
    x_copy(z, other).wait_recv()
    for step in near:
        w_copy(z, beside(step)).start()
    a_all(0, g_rows).wait_recv()
    h_rows[h] = g_rows[:, 0, :].astype(bf16)
    a_start(1, h_rows, h)
    sub = lax.broadcasted_iota(i32, (n_pcol, 128), 0) + prow * n_pcol
    found = jnp.where(block[0:1, :] == sub, offset[0:1, :], 0.0) + jnp.where(
        block[1:2, :] == sub, offset[1:2, :], 0.0
    )
    row_at = jnp.sum(found, axis=1, keepdims=True) + (
        lax.broadcasted_iota(i32, (n_pcol, 1), 0) * rows_dev
    ).astype(f32)
    chosen = jnp.zeros((n_pcol, trailing.shape[1]), f32)
    for part in range(T_PARTS):
        t_copy(part).wait()
        lane = lax.broadcasted_iota(i32, (n_pcol, part_rows), 1).astype(f32) + part * part_rows
        pick = jnp.where(lane == row_at, 1.0, 0.0).astype(bf16)
        chosen = chosen + jnp.dot(
            pick, t_buf[part * part_rows:(part + 1) * part_rows, :], preferred_element_type=f32
        )
    c_out[x_lo, y] = chosen.astype(bf16)
    c_x_copy(x_lo).start()
    for step in far:
        z_copy(beside(-step), z).wait_recv()
        x_copy(beside(-step), place).start()
    for step in near:
        z_copy(beside(-step), z).wait_recv()
    sib_copy(0, place).start()
    for step in range(1, n_y):
        c_y_copy(x_lo, y, 0, step).start()
    a_all(1, h_rows).wait_recv()
    work[:, :256] = jnp.dot(
        order[...], h_rows[...].reshape(256, 256), preferred_element_type=f32
    )

    def pass_chosen():
        c_x_copy(1 - x_lo).wait_recv()
        for step in range(1, n_y):
            c_y_copy(1 - x_lo, y, 1, step).start()

    def pass_far():
        for step in near:
            w_copy(beside(-step), z).wait_recv()
        for step in far:
            x_copy(beside(-step), other).wait_recv()
        sib_copy(1, other).start()

    hooks = {4: [pass_chosen], 8: [pass_far]}
    eliminate(work, lower_inv, 16, hooks)
    full_inv[...] = work[:, 256:]

    for step in range(1, n_y):
        at = lax.rem(y + n_y - step, n_y)
        c_y_copy(x_lo, at, 0, step).wait_recv()
        c_y_copy(1 - x_lo, at, 1, step).wait_recv()
    sib_copy(0, x_hi * 2 + 1 - core).wait_recv()
    sib_copy(1, (1 - x_hi) * 2 + 1 - core).wait_recv()

    for stage, ref in enumerate((g_rows, h_rows)):
        a_all(stage, ref).wait_send()
    for step in far + near:
        z_copy(z, beside(step)).wait_send()
    for step in near:
        w_copy(z, beside(step)).wait_send()
    for step in (0,) + far:
        x_copy(beside(-step), place).wait_send()
    sib_copy(0, place).wait_send()
    sib_copy(1, other).wait_send()
    c_x_copy(x_lo).wait_send()
    for step in range(1, n_y):
        c_y_copy(x_lo, y, 0, step).wait_send()
        c_y_copy(1 - x_lo, y, 1, step).wait_send()


def factor(n_prow, n_pcol, pivots, panels, trailing):
    rows_dev, width = panels.shape
    n_z, n_y = n_pcol // 4, n_prow // 2
    columns = trailing.shape[1]
    dma = pltpu.SemaphoreType.DMA
    vmem, hbm = pl.BlockSpec(memory_space=pltpu.VMEM), pl.BlockSpec(memory_space=pltpu.HBM)
    pivots, panels, trailing = (
        pltpu.with_memory_space_constraint(x, pltpu.HBM) for x in (pivots, panels, trailing)
    )
    return pl.pallas_call(
        functools.partial(factor_kernel, n_prow, n_pcol),
        out_shape=[
            jax.ShapeDtypeStruct((width, width), f32),
            jax.ShapeDtypeStruct((width, width), f32),
            jax.ShapeDtypeStruct((2, n_y, n_pcol, columns), bf16),
            jax.ShapeDtypeStruct((n_z, 4, rows_dev, width), bf16),
        ],
        in_specs=[hbm] * 3,
        out_specs=[vmem] * 4,
        scratch_shapes=[
            pltpu.VMEM(trailing.shape, bf16),
            pltpu.VMEM(pivots.shape, i32),
            pltpu.VMEM((2 * n_z, 1, width), f32),
            pltpu.VMEM((4 * n_y, 2 * n_z, width), bf16),
            pltpu.VMEM((width, 2 * width), f32),
            pltpu.VMEM((width, width), bf16),
            dma((T_PARTS,)), dma((2,)),
            dma((2,)), dma((2,)),
            dma((n_z,)), dma((n_z,)), dma((n_z,)), dma((n_z,)), dma((n_z,)), dma((n_z,)),
            dma((2,)), dma((2,)),
            dma((1 + 2 * n_y,)), dma((1 + 2 * n_y,)),
        ],
        compiler_params=pltpu.CompilerParams(
            collective_id=0, has_side_effects=True, vmem_limit_bytes=32 * 1024 * 1024
        ),
        name="factor_rows",
    )(pivots, panels, trailing)


def eliminate(work, lower_inv, extent, hooks):
    total = 256
    shape = (extent, 128)
    sub = lax.broadcasted_iota(i32, shape, 0)
    lanes = lax.broadcasted_iota(i32, (total, 128), 1)

    def across(x, k):
        return jnp.broadcast_to(x[k:k + 1, :], shape)

    def column(rows, at):
        piece, lane = divmod(at, 128)
        return jnp.broadcast_to(rows[piece][:, lane:lane + 1], shape)

    def load(first):
        return [work[first:first + extent, 128 * q:128 * q + 128] for q in range(4)]

    rows = load(0)
    for first in range(0, total, extent):
        for hook in hooks.get(first // extent, []):
            hook()
        piece, lane = divmod(first, 128)
        after = first + extent
        last = after >= total
        live = [q for q in range(4) if (q + 1) * 128 > after]
        columns = [column(rows, first + k) for k in range(extent)]
        if not last:
            ahead = load(after)
            ahead_columns = [column(ahead, first + k) for k in range(extent)]
        inverse = jnp.zeros(shape, f32)
        upper = [jnp.zeros(shape, f32)] * 2
        for k in range(extent):
            reciprocal = 1.0 / across(columns[k], k)
            factor = jnp.where(sub == k, 0.0, columns[k] * reciprocal)
            inverse = jnp.where(sub == k, reciprocal, inverse)
            upper = [jnp.where(sub == k, rows[2 + q], upper[q]) for q in range(2)]
            pivot_row = {q: across(rows[q], k) for q in live}
            pivot_columns = [across(columns[j], k) for j in range(k + 1, extent)]
            if not last:
                times = ahead_columns[k] * reciprocal
                for j in range(k + 1, extent):
                    ahead_columns[j] = ahead_columns[j] - times * pivot_columns[j - k - 1]
                for q in live:
                    ahead[q] = ahead[q] - times * pivot_row[q]
            for j in range(k + 1, extent):
                columns[j] = columns[j] - factor * pivot_columns[j - k - 1]
            for q in live:
                rows[q] = rows[q] - factor * pivot_row[q]
        rows = [x * inverse for x in rows]
        for q in range(2):
            lower_inv[first:after, 128 * q:128 * q + 128] = upper[q]
        group = work[:, 128 * piece:128 * piece + 128]
        high = group.astype(bf16).astype(f32)
        low = group - high
        second, third = (lane + extent) % 128, (lane + 2 * extent) % 128
        left = jnp.where(
            (lanes >= lane) & (lanes < lane + extent), high,
            jnp.where((lanes >= second) & (lanes < second + extent), pltpu.roll(low, extent, 1),
                      pltpu.roll(high, 2 * extent, 1)),
        ).astype(bf16)
        blank = jnp.zeros(shape, bf16)
        for pair in [live[:-2], live[-2:]] if len(live) > 2 else [live]:
            tiles = []
            for p in pair:
                xh, xl = split(rows[p])
                parts = [blank] * (128 // extent)
                parts[lane // extent], parts[second // extent], parts[third // extent] = xh, xh, xl
                tiles.append(jnp.concatenate(parts, axis=0))
            right = jnp.concatenate(tiles, axis=1) if len(tiles) > 1 else tiles[0]
            cs = slice(128 * pair[0], 128 * (pair[-1] + 1))
            for lo_row, hi_row in ((0, first), (after + extent, total)):
                if hi_row <= lo_row:
                    continue
                work[lo_row:hi_row, cs] = work[lo_row:hi_row, cs] - jnp.dot(
                    left[lo_row:hi_row], right, preferred_element_type=f32)
        for q in live:
            work[first:after, 128 * q:128 * q + 128] = rows[q]
        if not last:
            rows = ahead

def solve_kernel(
    lower_inv, full_inv, chosen, panels, trailing, updated, upper_rows, x_buf, u_buf, o_buf, o_sem, u_sem
):
    part_rows = trailing.shape[0] // OUT_PARTS

    def o_copy(part):
        at = pl.ds(part * part_rows, part_rows)
        return pltpu.make_async_copy(o_buf.at[at], updated.at[at], o_sem.at[part])

    def product(left, right):
        high, low = split(left)
        return jnp.dot(high, right, preferred_element_type=f32) + jnp.dot(
            low, right, preferred_element_type=f32
        )

    u_copy = pltpu.make_async_copy(u_buf, upper_rows, u_sem)
    x_buf[...] = product(full_inv[...], chosen[...]).astype(bf16)
    for part in range(OUT_PARTS):
        at = slice(part * part_rows, (part + 1) * part_rows)
        o_buf[at, :] = (
            trailing[at, :].astype(f32)
            - jnp.dot(panels[at, :], x_buf[...], preferred_element_type=f32)
        ).astype(bf16)
        o_copy(part).start()
        if part == OUT_PARTS // 2:
            u_buf[...] = product(lower_inv[...], chosen[...]).astype(bf16)
            u_copy.start()
    for part in range(OUT_PARTS):
        o_copy(part).wait()
    u_copy.wait()


def solve(lower_inv, full_inv, chosen, panels, trailing):
    width, columns = chosen.shape
    vmem = pl.BlockSpec(memory_space=pltpu.VMEM)
    return pl.pallas_call(
        solve_kernel,
        out_shape=[
            jax.ShapeDtypeStruct(trailing.shape, bf16),
            jax.ShapeDtypeStruct((width, columns), bf16),
        ],
        in_specs=[vmem] * 5,
        out_specs=[pl.BlockSpec(memory_space=pl.ANY)] * 2,
        scratch_shapes=[
            pltpu.VMEM((width, columns), bf16),
            pltpu.VMEM((width, columns), bf16),
            pltpu.VMEM(trailing.shape, bf16),
            pltpu.SemaphoreType.DMA((OUT_PARTS,)),
            pltpu.SemaphoreType.DMA,
        ],
        compiler_params=pltpu.CompilerParams(vmem_limit_bytes=32 * 1024 * 1024),
        name="solve_update",
    )(lower_inv, full_inv, chosen, panels, trailing)


def solution(mesh):
    n_prow, n_pcol = mesh.shape["prow"], mesh.shape["pcol"]

    def local(panels, pivots, trailing):
        lower_inv, full_inv, chosen, rows = factor(n_prow, n_pcol, pivots, panels, trailing)
        width = panels.shape[1]
        updated, upper_rows = solve(
            lower_inv, full_inv, chosen.reshape(width, trailing.shape[1]),
            rows.reshape(trailing.shape[0], width), trailing,
        )
        return updated, upper_rows

    return jax.shard_map(
        local,
        mesh=mesh,
        in_specs=(P(("prow", "pcol"), None), P(), P("prow", "pcol")),
        out_specs=(P("prow", "pcol"), P(None, "pcol")),
        check_vma=False,
    )
```

```python
import functools

import jax
import jax.numpy as jnp
from jax import lax
from jax.experimental import pallas as pl
from jax.experimental.pallas import tpu as pltpu
from jax.sharding import PartitionSpec as P

f32, bf16, i32 = jnp.float32, jnp.bfloat16, jnp.int32
MESH = pl.DeviceIdType.MESH
T_PARTS = 4
OUT_PARTS = 8


def split(x):
    high = x.astype(bf16)
    return high, (x - high.astype(f32)).astype(bf16)


def factor_kernel(
    n_prow, n_pcol, pivots, panels, trailing, lower_inv, full_inv, c_out, p_out,
    t_buf, piv_buf, g_rows, h_rows, work, order,
    t_sem, in_sem, a_send, a_recv, z_send, z_recv, x_send, x_recv, w_send, w_recv, sib_send, sib_recv,
    c_send, c_recv,
):
    n_z, n_y = n_pcol // 4, n_prow // 2
    prow, pcol = lax.axis_index("prow"), lax.axis_index("pcol")
    x_lo, y = prow // n_y, lax.rem(prow, n_y)
    z, place = pcol // 4, lax.rem(pcol, 4)
    x_hi, core = place // 2, lax.rem(place, 2)
    g, h = z * 2 + core, (x_lo * 2 + x_hi) * n_y + y
    other = (1 - x_hi) * 2 + core
    rows_dev = panels.shape[0]
    part_rows = trailing.shape[0] // T_PARTS

    def t_copy(part):
        at = pl.ds(part * part_rows, part_rows)
        return pltpu.make_async_copy(trailing.at[at], t_buf.at[at], t_sem.at[part])

    piv_copy = pltpu.make_async_copy(pivots, piv_buf, in_sem.at[0])
    own_copy = pltpu.make_async_copy(panels, p_out.at[z, place], in_sem.at[1])
    piv_copy.start()
    own_copy.start()
    for part in range(T_PARTS):
        t_copy(part).start()

    def g_peer(step):
        to_z, to_core = step
        at_z, at_core = lax.rem(z + to_z, n_z), lax.rem(core + to_core, 2)
        return {"prow": prow, "pcol": at_z * 4 + x_hi * 2 + at_core}

    def h_peer(step):
        to_hi, to_lo, to_y = step
        at_hi, at_lo = lax.rem(x_hi + to_hi, 2), lax.rem(x_lo + to_lo, 2)
        return {
            "prow": at_lo * n_y + lax.rem(y + to_y, n_y),
            "pcol": z * 4 + at_hi * 2 + core,
        }

    def y_peer(step):
        return {"prow": x_lo * n_y + lax.rem(y + step, n_y), "pcol": pcol}

    def hops(distance, around):
        return min(distance, around - distance)

    g_steps = sorted(
        ((to_z, to_core) for to_z in range(n_z) for to_core in range(2) if to_z + to_core),
        key=lambda step: (-hops(step[0], n_z), step),
    )
    h_steps = sorted(
        ((hi, lo, to_y) for hi in range(2) for lo in range(2) for to_y in range(n_y)
         if hi + lo + to_y),
        key=lambda step: (-hops(step[2], n_y) - (0, 1, 2, 1)[2 * step[0] + step[1]], step),
    )
    groups = ((g_peer, g_steps), (h_peer, h_steps))
    barrier = pltpu.get_barrier_semaphore()
    for peer, steps in groups:
        for step in steps:
            pl.semaphore_signal(barrier, inc=1, device_id=peer(step), device_id_type=MESH)

    piv_copy.wait()
    pivot = piv_buf[...]
    block = pivot // rows_dev
    offset = (pivot - block * rows_dev).astype(f32)
    own = jnp.where(block == prow * n_pcol + pcol, offset, 0.0)
    own_offset = jnp.sum(jnp.sum(own, axis=0, keepdims=True), axis=1, keepdims=True)
    lane = lax.broadcasted_iota(i32, (16, rows_dev), 1).astype(f32)
    pick = jnp.where(lane == own_offset, 1.0, 0.0).astype(bf16)
    own_copy.wait()
    own_row = jnp.dot(pick, p_out[z, place], preferred_element_type=f32)
    g_rows[g] = own_row[0:1, :]
    pl.semaphore_wait(barrier, 2 * n_z - 1 + 4 * n_y - 1)

    def a_copy(stage, ref, slot, target):
        return pltpu.make_async_remote_copy(
            src_ref=ref.at[slot], dst_ref=ref.at[slot],
            send_sem=a_send.at[stage], recv_sem=a_recv.at[stage],
            device_id=target, device_id_type=MESH,
        )

    def a_start(stage, ref, slot):
        peer, steps = groups[stage]
        for step in steps:
            a_copy(stage, ref, slot, peer(step)).start()

    def a_all(stage, ref):
        return a_copy(stage, ref, pl.ds(0, len(groups[stage][1])), y_peer(1))

    def z_copy(slot, target):
        return pltpu.make_async_remote_copy(
            src_ref=p_out.at[slot, place], dst_ref=p_out.at[slot, place],
            send_sem=z_send.at[target], recv_sem=z_recv.at[slot],
            device_id={"prow": prow, "pcol": target * 4 + place}, device_id_type=MESH,
        )

    def x_copy(slot, at_place):
        return pltpu.make_async_remote_copy(
            src_ref=p_out.at[slot, at_place], dst_ref=p_out.at[slot, at_place],
            send_sem=x_send.at[slot], recv_sem=x_recv.at[slot],
            device_id={"prow": prow, "pcol": z * 4 + (1 - x_hi) * 2 + core},
            device_id_type=MESH,
        )

    def w_copy(slot, target):
        return pltpu.make_async_remote_copy(
            src_ref=p_out.at[slot, other], dst_ref=p_out.at[slot, other],
            send_sem=w_send.at[target], recv_sem=w_recv.at[slot],
            device_id={"prow": prow, "pcol": target * 4 + place}, device_id_type=MESH,
        )

    def sib_copy(slot, at_place):
        return pltpu.make_async_remote_copy(
            src_ref=p_out.at[:, at_place], dst_ref=p_out.at[:, at_place],
            send_sem=sib_send.at[slot], recv_sem=sib_recv.at[slot],
            device_id={"prow": prow, "pcol": z * 4 + x_hi * 2 + (1 - core)},
            device_id_type=MESH,
        )

    def c_copy(at_x, at_y, number, slot, target):
        return pltpu.make_async_remote_copy(
            src_ref=c_out.at[at_x, at_y], dst_ref=c_out.at[at_x, at_y],
            send_sem=c_send.at[number], recv_sem=c_recv.at[slot],
            device_id=target, device_id_type=MESH,
        )

    x_other = {"prow": (1 - x_lo) * n_y + y, "pcol": pcol}

    def c_x_copy(at_x):
        return c_copy(at_x, y, 0, 0, x_other)

    def c_y_copy(at_x, at_y, number, step):
        return c_copy(
            at_x, at_y, 1 + number * n_y + step, 1 + number * n_y + at_y, y_peer(step)
        )

    def beside(step):
        return lax.rem(z + step + n_z, n_z)

    a_start(0, g_rows, g)
    near, far = (1, -1, 2, -2), (3, -3, 4)
    x_copy(z, place).start()
    for step in far + near:
        z_copy(z, beside(step)).start()
    at_prow, at_pcol = block // n_pcol, lax.rem(block, n_pcol)
    at_x = (at_prow // n_y) * 2 + lax.rem(at_pcol, 4) // 2
    at_h = at_x * n_y + lax.rem(at_prow, n_y)
    a_at = (at_h * n_z + at_pcol // 4) * 2 + lax.rem(at_pcol, 2)
    for half in range(2):
        for target, where_from in ((work, block), (order, a_at)):
            value = where_from[half:half + 1, :].astype(f32)
            turned = jnp.transpose(jnp.broadcast_to(value, (128, 128)))
            for part in range(2):
                lane = lax.broadcasted_iota(i32, (128, 128), 1).astype(f32) + 128 * part
                first = 256 + 128 * part if target is work else 128 * part
                target[128 * half:128 * half + 128, first:first + 128] = jnp.where(
                    turned == lane, 1.0, 0.0
                ).astype(target.dtype)
    x_copy(z, other).wait_recv()
    for step in near:
        w_copy(z, beside(step)).start()
    a_all(0, g_rows).wait_recv()
    h_rows[h] = g_rows[:, 0, :].astype(bf16)
    a_start(1, h_rows, h)
    sub = lax.broadcasted_iota(i32, (n_pcol, 128), 0) + prow * n_pcol
    found = jnp.where(block[0:1, :] == sub, offset[0:1, :], 0.0) + jnp.where(
        block[1:2, :] == sub, offset[1:2, :], 0.0
    )
    row_at = jnp.sum(found, axis=1, keepdims=True) + (
        lax.broadcasted_iota(i32, (n_pcol, 1), 0) * rows_dev
    ).astype(f32)
    chosen = jnp.zeros((n_pcol, trailing.shape[1]), f32)
    for part in range(T_PARTS):
        t_copy(part).wait()
        lane = lax.broadcasted_iota(i32, (n_pcol, part_rows), 1).astype(f32) + part * part_rows
        pick = jnp.where(lane == row_at, 1.0, 0.0).astype(bf16)
        chosen = chosen + jnp.dot(
            pick, t_buf[part * part_rows:(part + 1) * part_rows, :], preferred_element_type=f32
        )
    c_out[x_lo, y] = chosen.astype(bf16)
    c_x_copy(x_lo).start()
    for step in far:
        z_copy(beside(-step), z).wait_recv()
        x_copy(beside(-step), place).start()
    for step in near:
        z_copy(beside(-step), z).wait_recv()
    sib_copy(0, place).start()
    for step in range(1, n_y):
        c_y_copy(x_lo, y, 0, step).start()
    a_all(1, h_rows).wait_recv()
    work[:, :256] = jnp.dot(
        order[...], h_rows[...].reshape(256, 256), preferred_element_type=f32
    )

    def pass_chosen():
        c_x_copy(1 - x_lo).wait_recv()
        for step in range(1, n_y):
            c_y_copy(1 - x_lo, y, 1, step).start()

    def pass_far():
        for step in near:
            w_copy(beside(-step), z).wait_recv()
        for step in far:
            x_copy(beside(-step), other).wait_recv()
        sib_copy(1, other).start()

    hooks = {4: [pass_chosen], 8: [pass_far]}
    eliminate(work, lower_inv, 16, hooks)
    full_inv[...] = work[:, 256:]

    for step in range(1, n_y):
        at = lax.rem(y + n_y - step, n_y)
        c_y_copy(x_lo, at, 0, step).wait_recv()
        c_y_copy(1 - x_lo, at, 1, step).wait_recv()
    sib_copy(0, x_hi * 2 + 1 - core).wait_recv()
    sib_copy(1, (1 - x_hi) * 2 + 1 - core).wait_recv()

    for stage, ref in enumerate((g_rows, h_rows)):
        a_all(stage, ref).wait_send()
    for step in far + near:
        z_copy(z, beside(step)).wait_send()
    for step in near:
        w_copy(z, beside(step)).wait_send()
    for step in (0,) + far:
        x_copy(beside(-step), place).wait_send()
    sib_copy(0, place).wait_send()
    sib_copy(1, other).wait_send()
    c_x_copy(x_lo).wait_send()
    for step in range(1, n_y):
        c_y_copy(x_lo, y, 0, step).wait_send()
        c_y_copy(1 - x_lo, y, 1, step).wait_send()


def factor(n_prow, n_pcol, pivots, panels, trailing):
    rows_dev, width = panels.shape
    n_z, n_y = n_pcol // 4, n_prow // 2
    columns = trailing.shape[1]
    dma = pltpu.SemaphoreType.DMA
    vmem, hbm = pl.BlockSpec(memory_space=pltpu.VMEM), pl.BlockSpec(memory_space=pltpu.HBM)
    pivots, panels, trailing = (
        pltpu.with_memory_space_constraint(x, pltpu.HBM) for x in (pivots, panels, trailing)
    )
    return pl.pallas_call(
        functools.partial(factor_kernel, n_prow, n_pcol),
        out_shape=[
            jax.ShapeDtypeStruct((width, width), f32),
            jax.ShapeDtypeStruct((width, width), f32),
            jax.ShapeDtypeStruct((2, n_y, n_pcol, columns), bf16),
            jax.ShapeDtypeStruct((n_z, 4, rows_dev, width), bf16),
        ],
        in_specs=[hbm] * 3,
        out_specs=[vmem] * 4,
        scratch_shapes=[
            pltpu.VMEM(trailing.shape, bf16),
            pltpu.VMEM(pivots.shape, i32),
            pltpu.VMEM((2 * n_z, 1, width), f32),
            pltpu.VMEM((4 * n_y, 2 * n_z, width), bf16),
            pltpu.VMEM((width, 2 * width), f32),
            pltpu.VMEM((width, width), bf16),
            dma((T_PARTS,)), dma((2,)),
            dma((2,)), dma((2,)),
            dma((n_z,)), dma((n_z,)), dma((n_z,)), dma((n_z,)), dma((n_z,)), dma((n_z,)),
            dma((2,)), dma((2,)),
            dma((1 + 2 * n_y,)), dma((1 + 2 * n_y,)),
        ],
        compiler_params=pltpu.CompilerParams(
            collective_id=0, has_side_effects=True, vmem_limit_bytes=32 * 1024 * 1024
        ),
        name="factor_rows",
    )(pivots, panels, trailing)


def eliminate(work, lower_inv, extent, hooks):
    total = 256
    shape = (extent, 128)
    sub = lax.broadcasted_iota(i32, shape, 0)
    lanes = lax.broadcasted_iota(i32, (total, 128), 1)

    def across(x, k):
        return jnp.broadcast_to(x[k:k + 1, :], shape)

    def column(rows, at):
        piece, lane = divmod(at, 128)
        return jnp.broadcast_to(rows[piece][:, lane:lane + 1], shape)

    def load(first):
        return [work[first:first + extent, 128 * q:128 * q + 128] for q in range(4)]

    rows = load(0)
    for first in range(0, total, extent):
        for hook in hooks.get(first // extent, []):
            hook()
        piece, lane = divmod(first, 128)
        after = first + extent
        last = after >= total
        live = [q for q in range(4) if (q + 1) * 128 > after]
        columns = [column(rows, first + k) for k in range(extent)]
        if not last:
            ahead = load(after)
            ahead_columns = [column(ahead, first + k) for k in range(extent)]
        inverse = jnp.zeros(shape, f32)
        upper = [jnp.zeros(shape, f32)] * 2
        for k in range(extent):
            reciprocal = 1.0 / across(columns[k], k)
            factor = jnp.where(sub == k, 0.0, columns[k] * reciprocal)
            inverse = jnp.where(sub == k, reciprocal, inverse)
            upper = [jnp.where(sub == k, rows[2 + q], upper[q]) for q in range(2)]
            pivot_row = {q: across(rows[q], k) for q in live}
            pivot_columns = [across(columns[j], k) for j in range(k + 1, extent)]
            if not last:
                times = ahead_columns[k] * reciprocal
                for j in range(k + 1, extent):
                    ahead_columns[j] = ahead_columns[j] - times * pivot_columns[j - k - 1]
                for q in live:
                    ahead[q] = ahead[q] - times * pivot_row[q]
            for j in range(k + 1, extent):
                columns[j] = columns[j] - factor * pivot_columns[j - k - 1]
            for q in live:
                rows[q] = rows[q] - factor * pivot_row[q]
        rows = [x * inverse for x in rows]
        for q in range(2):
            lower_inv[first:after, 128 * q:128 * q + 128] = upper[q]
        group = work[:, 128 * piece:128 * piece + 128]
        high = group.astype(bf16).astype(f32)
        low = group - high
        second, third = (lane + extent) % 128, (lane + 2 * extent) % 128
        left = jnp.where(
            (lanes >= lane) & (lanes < lane + extent), high,
            jnp.where((lanes >= second) & (lanes < second + extent), pltpu.roll(low, extent, 1),
                      pltpu.roll(high, 2 * extent, 1)),
        ).astype(bf16)
        blank = jnp.zeros(shape, bf16)
        for pair in [live[:-2], live[-2:]] if len(live) > 2 else [live]:
            tiles = []
            for p in pair:
                xh, xl = split(rows[p])
                parts = [blank] * (128 // extent)
                parts[lane // extent], parts[second // extent], parts[third // extent] = xh, xh, xl
                tiles.append(jnp.concatenate(parts, axis=0))
            right = jnp.concatenate(tiles, axis=1) if len(tiles) > 1 else tiles[0]
            cs = slice(128 * pair[0], 128 * (pair[-1] + 1))
            for lo_row, hi_row in ((0, first), (after + extent, total)):
                if hi_row <= lo_row:
                    continue
                work[lo_row:hi_row, cs] = work[lo_row:hi_row, cs] - jnp.dot(
                    left[lo_row:hi_row], right, preferred_element_type=f32)
        for q in live:
            work[first:after, 128 * q:128 * q + 128] = rows[q]
        if not last:
            rows = ahead

def solve_kernel(
    lower_inv, full_inv, chosen, panels, trailing, updated, upper_rows, x_buf, u_buf, o_buf, o_sem, u_sem
):
    part_rows = trailing.shape[0] // OUT_PARTS

    def o_copy(part):
        at = pl.ds(part * part_rows, part_rows)
        return pltpu.make_async_copy(o_buf.at[at], updated.at[at], o_sem.at[part])

    def product(left, right):
        high, low = split(left)
        return jnp.dot(high, right, preferred_element_type=f32) + jnp.dot(
            low, right, preferred_element_type=f32
        )

    u_copy = pltpu.make_async_copy(u_buf, upper_rows, u_sem)
    x_buf[...] = product(full_inv[...], chosen[...]).astype(bf16)
    for part in range(OUT_PARTS):
        at = slice(part * part_rows, (part + 1) * part_rows)
        o_buf[at, :] = (
            trailing[at, :].astype(f32)
            - jnp.dot(panels[at, :], x_buf[...], preferred_element_type=f32)
        ).astype(bf16)
        o_copy(part).start()
        if part == OUT_PARTS // 2:
            u_buf[...] = product(lower_inv[...], chosen[...]).astype(bf16)
            u_copy.start()
    for part in range(OUT_PARTS):
        o_copy(part).wait()
    u_copy.wait()


def solve(lower_inv, full_inv, chosen, panels, trailing):
    width, columns = chosen.shape
    vmem = pl.BlockSpec(memory_space=pltpu.VMEM)
    return pl.pallas_call(
        solve_kernel,
        out_shape=[
            jax.ShapeDtypeStruct(trailing.shape, bf16),
            jax.ShapeDtypeStruct((width, columns), bf16),
        ],
        in_specs=[vmem] * 5,
        out_specs=[pl.BlockSpec(memory_space=pl.ANY)] * 2,
        scratch_shapes=[
            pltpu.VMEM((width, columns), bf16),
            pltpu.VMEM((width, columns), bf16),
            pltpu.VMEM(trailing.shape, bf16),
            pltpu.SemaphoreType.DMA((OUT_PARTS,)),
            pltpu.SemaphoreType.DMA,
        ],
        compiler_params=pltpu.CompilerParams(vmem_limit_bytes=32 * 1024 * 1024),
        name="solve_update",
    )(lower_inv, full_inv, chosen, panels, trailing)


def solution(mesh):
    n_prow, n_pcol = mesh.shape["prow"], mesh.shape["pcol"]

    def local(panels, pivots, trailing):
        lower_inv, full_inv, chosen, rows = factor(n_prow, n_pcol, pivots, panels, trailing)
        width = panels.shape[1]
        updated, upper_rows = solve(
            lower_inv, full_inv, chosen.reshape(width, trailing.shape[1]),
            rows.reshape(trailing.shape[0], width), trailing,
        )
        return updated, upper_rows

    return jax.shard_map(
        local,
        mesh=mesh,
        in_specs=(P(("prow", "pcol"), None), P(), P("prow", "pcol")),
        out_specs=(P("prow", "pcol"), P(None, "pcol")),
        check_vma=False,
    )
```
